32 devices in a mesh: groups: 2 (over y), seq: 8 (over z, x), head: 2 (over core).
Axes of the slice: x: 2, y: 2, z: 4, core: 2. Of those that a mesh axis runs over, the one named last changes fastest.
Arguments:
- text_query_rows: bfloat16 [2048, 8192], P(('groups', 'seq'), 'head'), parts along dimension 0, may hold values from -40 to 40, as said below
- text_key_value: bfloat16 [2, 2048, 1024], P(None, ('groups', 'seq'), 'head'), parts along dimension 1, may hold values from -4 to 4, as said below
- doc_ids: int32 [2048], P(('groups', 'seq')), parts along dimension 0, may hold values from 0 to 3, never falling along the last dimension, each value on 1 to 512 neighbouring positions
- tile_span: int32 [2048, 2], P(('groups', 'seq')), parts along dimension 0, may hold values from 0 to 8, as said below
- vision_hidden: bfloat16 [4096, 1280], P(('groups', 'seq')), parts along dimension 0, may hold values from -6 to 6
- vision_qkv: bfloat16 [3, 4096, 1280], P(None, ('groups', 'seq'), 'head'), parts along dimension 1, may hold values from -6 to 6, as said below
- vision_out_weight: bfloat16 [1280, 1280], P('head'), may hold values from -0.625 to 0.625
- cross_keyvalue_weight: bfloat16 [1280, 2, 1024], P('seq', None, 'head'), may hold values from -0.15625 to 0.15625
- cross_gate: float32 [64], P('head'), may hold values from -1.5 to 1.5
Outputs:
- attention_out: bfloat16 [2048, 8192], P(('groups', 'seq'), 'head'), parts along dimension 0
The draws below stay inside these ranges and needn't reach their ends.
There are 2 independent parts, one for each index of `groups`. The reference program is written for one: setup_inputs(seed, part) draws one part's arguments, and reference() takes and returns one part's arrays. A program takes and returns all parts, laid end to end along the dimension named above; an argument that names none is the same for every part. Nothing has to cross between parts.
Inputs may be any that keep to these rules, and one draw needn't show every extreme that they name: `tile_span`: each text token's span is an interval of the tiles of its own block b = p // 128 and of block b - 1 (first <= second, both between b - 1 and b + 1, never below 0); it may be empty. `doc_ids`: never falling along the document; each segment holds 1 to 512 tokens. `text_query_rows`: real values. `text_key_value`: real values. `vision_qkv`: real values.
All inputs are finite; a program needn't handle non-finite values.
Results may differ from the reference program's by a relative error of at most 0.024.
Values may be sent and summed in bfloat16 or wider, within the bound.
No kernel may reach another device: no remote copies, remote signals or barrier semaphores. Data moves between devices by JAX's collectives and lax.ppermute only.
A program may use at most 64 MiB of HBM per device.

```python
import math
import jax
import jax.numpy as jnp
import numpy as np
from jax import lax

QUERY_HEADS = 64
KEY_VALUE_HEADS = 8
HEAD_SIZE = 128
VISION_LAYER_WIDTH = 1280
VH = 16
VHD = 80
BLOCK_TOKENS = 128
TILE_WINDOW_ROWS = 256
WINDOW_BLOCKS = 2
DOCUMENT_TOKENS = 1024
IMG_TOK = 2048
DOCS = 4
N_SEQ = 8


def text_pair(key):
    key_value_random = jax.random.fold_in(key, 7)
    query_key = jax.random.fold_in(key, 8)
    key_value = jnp.clip(jax.random.normal(key_value_random, (2, DOCUMENT_TOKENS, KEY_VALUE_HEADS * HEAD_SIZE), jnp.float32), -4.0, 4.0)
    query_rows = jnp.clip(jax.random.normal(query_key, (DOCUMENT_TOKENS, QUERY_HEADS * HEAD_SIZE), jnp.float32), -4.0, 4.0)
    return (query_rows, key_value)


def draw_text_query_rows(key, part):
    return text_pair(key)[0].astype(jnp.bfloat16)


def draw_text_key_value(key, part):
    return text_pair(key)[1].astype(jnp.bfloat16)


def draw_vision_qkv(key, part):
    result = jnp.clip(jax.random.normal(jax.random.fold_in(key, 21), (3, IMG_TOK, VISION_LAYER_WIDTH), jnp.float32), -6.0, 6.0)
    return result.astype(jnp.bfloat16)


def draw_tile_span(key, part):
    positions = jnp.arange(DOCUMENT_TOKENS, dtype=jnp.int32)
    block_ids = positions // BLOCK_TOKENS
    modes = jax.random.randint(jax.random.fold_in(key, 3), (DOCUMENT_TOKENS,), 0, 4)
    low_tile = jnp.where((modes == 1) | (modes == 3), block_ids - 1, block_ids)
    high_tile = jnp.where((modes == 1) | (modes == 0), block_ids, block_ids + 1)
    low_tile = jnp.maximum(low_tile, 0)
    high_tile = jnp.maximum(high_tile, low_tile)
    return jnp.stack([low_tile, high_tile], axis=1).astype(jnp.int32)


def shard_levels(own_key, dims, shards, low, largest):
    loudness, own = 1.0, jax.random.fold_in(own_key, 6)
    for dim, blocks in shards:
        steps = jnp.exp(jax.random.uniform(jax.random.fold_in(own, dim), (blocks,), jnp.float32, low / len(shards), largest / len(shards)))
        loudness = loudness * jnp.repeat(steps, dims[dim] // blocks).reshape([-1 if axis == dim else 1 for axis in range(len(dims))])
    return loudness


def split_up(number_of, total, bound, skew):
    weights = [(1 << 20) // math.isqrt(grade ** skew) + 1 for grade in range(2, number_of + 1)]
    spare, counts = total - bound - (number_of - 1), [1] * (number_of - 1)
    while spare > 0:
        movable = [i for i in range(number_of - 1) if counts[i] < bound]
        pool, left = sum([weights[i] for i in movable]), spare
        for i in movable:
            extra = min(bound - counts[i], max(1, left * weights[i] // pool), spare)
            counts[i] = counts[i] + extra
            spare = spare - extra
    return np.array([bound] + counts)


def uneven_parts(rng, number_of, total, limit, lean):
    if number_of == 2:
        one = jax.random.randint(rng, (), max(1, total - limit), min(limit, total - 1) + 1)
        return jnp.stack([one, total - one])
    lengths = jnp.asarray(split_up(number_of, total, limit, lean), jnp.int32)
    pairs = (number_of - 1) // 2
    source_of, taker = lengths[1:1 + 2 * pairs:2], lengths[2:2 + 2 * pairs:2]
    room = jnp.minimum(source_of - 1, limit - taker)
    moved = jax.random.randint(jax.random.fold_in(rng, 1), (pairs,), 0, 1 << 20) % (room + 1)
    lengths = lengths.at[1:1 + 2 * pairs:2].set(source_of - moved).at[2:2 + 2 * pairs:2].set(taker + moved)
    return lengths[jax.random.permutation(jax.random.fold_in(rng, 2), number_of)]


def normal_values(own_key, extent, scale, most, cuts=(), kind=jnp.bfloat16):
    values = jax.random.normal(own_key, extent, jnp.float32) * scale
    if len(cuts) > 0:
        values = shard_levels(own_key, extent, cuts, -0.22, 0.18) * values
    return jnp.clip(values, min=-most, max=most).astype(kind)


def setup_inputs(seed: int = 0, part: int = 0) -> dict:
    arg_keys = jax.random.split(jax.random.key(seed), 10)
    part_keys = jax.random.split(jax.random.fold_in(arg_keys[9], part), 10)
    return {
        "text_query_rows": draw_text_query_rows(jax.random.fold_in(jax.random.fold_in(arg_keys[9], part), 71), part),
        "text_key_value": draw_text_key_value(jax.random.fold_in(jax.random.fold_in(arg_keys[9], part), 71), part),
        "doc_ids": jnp.searchsorted(jnp.cumsum(uneven_parts(part_keys[2], DOCS, DOCUMENT_TOKENS, 4 * BLOCK_TOKENS, 0)), jnp.arange(DOCUMENT_TOKENS), side="right").astype(jnp.int32),
        "tile_span": draw_tile_span(jax.random.fold_in(jax.random.fold_in(arg_keys[9], part), 71), part),
        "vision_hidden": normal_values(part_keys[4], (IMG_TOK, VISION_LAYER_WIDTH), 1.0, 6.0, ((0, 8),)),
        "vision_qkv": draw_vision_qkv(jax.random.fold_in(jax.random.fold_in(arg_keys[9], part), 71), part),
        "vision_out_weight": normal_values(arg_keys[6], (VISION_LAYER_WIDTH, VISION_LAYER_WIDTH), (VISION_LAYER_WIDTH // 16) ** -0.5, 0.625, ((0, 2),)),
        "cross_keyvalue_weight": normal_values(arg_keys[7], (VISION_LAYER_WIDTH, 2, KEY_VALUE_HEADS * HEAD_SIZE), VISION_LAYER_WIDTH ** -0.5, 0.15625, ((0, 8), (2, 2))),
        "cross_gate": jnp.clip(jax.random.uniform(arg_keys[8], (QUERY_HEADS,), jnp.float32, -1.5, 1.5) * shard_levels(arg_keys[8], (QUERY_HEADS,), ((0, 2),), -0.4, 0.0), -1.5, 1.5),
    }


def attend_heads(query_rows, keys, allowed_mask):
    scores = jnp.einsum('tgrd,kgd->grtk', query_rows, keys, preferred_element_type=jnp.float32) / math.sqrt(HEAD_SIZE)
    scores = jnp.where(allowed_mask[None, None], scores, -1e+30)
    return jax.nn.softmax(scores, axis=-1)

def reference(text_query_rows, text_key_value, doc_ids, tile_span, vision_hidden, vision_qkv, vision_out_weight, cross_keyvalue_weight, cross_gate):
    query_group_ratio = QUERY_HEADS // KEY_VALUE_HEADS

    def vision_tile(tile_number):
        tile_rows = lax.dynamic_slice_in_dim(vision_qkv, tile_number * TILE_WINDOW_ROWS, TILE_WINDOW_ROWS, 1).astype(jnp.float32)
        query_rows = tile_rows[0].reshape(TILE_WINDOW_ROWS, VH, VHD)
        keys = tile_rows[1].reshape(TILE_WINDOW_ROWS, VH, VHD)
        values = tile_rows[2].reshape(TILE_WINDOW_ROWS, VH, VHD)
        scores = jnp.einsum('qhd,khd->hqk', query_rows, keys) / math.sqrt(VHD)
        weights = jax.nn.softmax(scores, axis=-1).astype(jnp.bfloat16)
        mixed_heads = jnp.einsum('hqk,khd->qhd', weights.astype(jnp.float32), values)
        return mixed_heads.astype(jnp.bfloat16).reshape(TILE_WINDOW_ROWS, VISION_LAYER_WIDTH)
    vision_attn = lax.map(vision_tile, jnp.arange(N_SEQ, dtype=jnp.int32)).reshape(IMG_TOK, VISION_LAYER_WIDTH)
    vision_mixed = vision_hidden.astype(jnp.float32) + jnp.dot(vision_attn, vision_out_weight, preferred_element_type=jnp.float32)
    image_norm = (vision_mixed * lax.rsqrt(lax.optimization_barrier(jnp.mean(vision_mixed * vision_mixed, axis=-1, keepdims=True)) + 1e-05)).astype(jnp.bfloat16)
    image_key_value = jnp.einsum('ic,cjf->ijf', image_norm.astype(jnp.float32), cross_keyvalue_weight.astype(jnp.float32)).astype(jnp.bfloat16)
    padded_key_value = jnp.concatenate([jnp.zeros((2, WINDOW_BLOCKS * BLOCK_TOKENS, KEY_VALUE_HEADS * HEAD_SIZE), text_key_value.dtype), text_key_value], axis=1)
    pad_docs = jnp.concatenate([jnp.zeros((WINDOW_BLOCKS * BLOCK_TOKENS,), jnp.int32), doc_ids], axis=0)
    padded_image = jnp.concatenate([jnp.zeros((TILE_WINDOW_ROWS, 2, KEY_VALUE_HEADS * HEAD_SIZE), image_key_value.dtype), image_key_value], axis=0)
    gate_cols = jnp.repeat(jnp.tanh(cross_gate), HEAD_SIZE)

    def text_block(block_number):
        starting_row = block_number * BLOCK_TOKENS
        query_rows = lax.dynamic_slice_in_dim(text_query_rows, starting_row, BLOCK_TOKENS, 0).astype(jnp.float32).reshape(BLOCK_TOKENS, KEY_VALUE_HEADS, query_group_ratio, HEAD_SIZE)
        key_value_pairs = lax.dynamic_slice_in_dim(padded_key_value, starting_row, (WINDOW_BLOCKS + 1) * BLOCK_TOKENS, 1).astype(jnp.float32)
        key_docs = lax.dynamic_slice_in_dim(pad_docs, starting_row, (WINDOW_BLOCKS + 1) * BLOCK_TOKENS, 0)
        own_docs = lax.dynamic_slice_in_dim(doc_ids, starting_row, BLOCK_TOKENS, 0)
        key_pos = starting_row - WINDOW_BLOCKS * BLOCK_TOKENS + jnp.arange((WINDOW_BLOCKS + 1) * BLOCK_TOKENS, dtype=jnp.int32)
        query_pos = starting_row + jnp.arange(BLOCK_TOKENS, dtype=jnp.int32)
        allowed_mask = (key_docs[None, :] == own_docs[:, None]) & (key_pos[None, :] <= query_pos[:, None]) & (key_pos[None, :] >= 0)
        self_attention_weights = attend_heads(query_rows, key_value_pairs[0].reshape(-1, KEY_VALUE_HEADS, HEAD_SIZE), allowed_mask).astype(jnp.bfloat16)
        self_output = jnp.einsum('ycmq,qyb->mycb', self_attention_weights.astype(jnp.float32), key_value_pairs[1].reshape(-1, KEY_VALUE_HEADS, HEAD_SIZE)).reshape(BLOCK_TOKENS, QUERY_HEADS * HEAD_SIZE)
        image_token_rows = lax.dynamic_slice_in_dim(padded_image, block_number * TILE_WINDOW_ROWS, 2 * TILE_WINDOW_ROWS, 0).astype(jnp.float32)
        tile_ids = block_number - 1 + jnp.arange(2 * TILE_WINDOW_ROWS, dtype=jnp.int32) // TILE_WINDOW_ROWS
        span_rows = lax.dynamic_slice_in_dim(tile_span, starting_row, BLOCK_TOKENS, 0)
        low_tile = span_rows[:, 0]
        high_tile = span_rows[:, 1]
        visible_mask = (tile_ids[None, :] >= low_tile[:, None]) & (tile_ids[None, :] < high_tile[:, None])
        image_present = (high_tile > low_tile).astype(jnp.float32)
        cross_probabilities = attend_heads(query_rows, image_token_rows[:, 0].reshape(-1, KEY_VALUE_HEADS, HEAD_SIZE), visible_mask) * image_present[None, None, :, None]
        cross_probabilities = cross_probabilities.astype(jnp.bfloat16)
        cross_output = jnp.einsum('ycmq,qyb->mycb', cross_probabilities.astype(jnp.float32), image_token_rows[:, 1].reshape(-1, KEY_VALUE_HEADS, HEAD_SIZE)).reshape(BLOCK_TOKENS, QUERY_HEADS * HEAD_SIZE)
        return (self_output + gate_cols[None, :] * cross_output).astype(jnp.bfloat16)
    outputs = lax.map(text_block, jnp.arange(N_SEQ, dtype=jnp.int32))
    return outputs.reshape(DOCUMENT_TOKENS, QUERY_HEADS * HEAD_SIZE)
```

```python
import functools
import math

import jax
import jax.numpy as jnp
from jax import lax
from jax.experimental import pallas as pl
from jax.experimental.pallas import tpu as pltpu
from jax.sharding import PartitionSpec as P

HEAD_SIZE = 128
VHD = 80
LANES = 128
WINDOW_BLOCKS = 2
ID_ROWS = 16
NEG = -1e30
LOG2E = math.log2(math.e)
F32 = jnp.float32
BF16 = jnp.bfloat16
VMEM_LIMIT = 40 * 1024 * 1024


def dot_t(a, b):
    return lax.dot_general(a, b, (((1,), (1,)), ((), ())), preferred_element_type=F32)


def dot_n(a, b):
    return lax.dot_general(a, b, (((1,), (0,)), ((), ())), preferred_element_type=F32)


def column_of(row):
    n = row.shape[1]
    at = lax.broadcasted_iota(jnp.int32, (n, n), 0) == lax.broadcasted_iota(jnp.int32, (n, n), 1)
    return jnp.sum(jnp.where(at, row, 0.0), axis=1, keepdims=True)


def call(kernel, out_shape, args, smem=0, scratch=(), flops=0, transcendentals=0):
    outs = out_shape if isinstance(out_shape, (tuple, list)) else (out_shape,)
    moved = sum(a.size * a.dtype.itemsize for a in args) + sum(
        math.prod(o.shape) * jnp.dtype(o.dtype).itemsize for o in outs
    )
    single = not isinstance(out_shape, (tuple, list))
    vmem = pl.BlockSpec(memory_space=pltpu.VMEM)
    return pl.pallas_call(
        kernel,
        out_shape=out_shape,
        in_specs=[pl.BlockSpec(memory_space=pltpu.SMEM)] * smem + [vmem] * (len(args) - smem),
        out_specs=vmem if single else [vmem] * len(outs),
        scratch_shapes=list(scratch),
        compiler_params=pltpu.CompilerParams(vmem_limit_bytes=VMEM_LIMIT),
        cost_estimate=pl.CostEstimate(
            flops=flops, bytes_accessed=moved, transcendentals=transcendentals
        ),
    )(*args)


def vision_kernel(qkv, out):
    rows, cols = out.shape
    tiles = cols // LANES
    acc = [None] * tiles
    scale = LOG2E / math.sqrt(VHD)
    for head in range(cols // VHD):
        first, last = head * VHD, (head + 1) * VHD
        t0, t1 = first // LANES, -(-last // LANES)
        lanes = slice(t0 * LANES, t1 * LANES)
        lane = lax.broadcasted_iota(jnp.int32, (rows, (t1 - t0) * LANES), 1) + t0 * LANES
        mine = (lane >= first) & (lane < last)
        q = jnp.where(mine, qkv[0, :, lanes], jnp.zeros((), BF16))
        v = jnp.where(mine, qkv[2, :, lanes], jnp.zeros((), BF16))
        s = dot_t(q, qkv[1, :, lanes])
        p = jnp.exp2((s - jnp.max(s, axis=1, keepdims=True)) * scale)
        total = jnp.sum(p, axis=1, keepdims=True)
        o = dot_n(p.astype(BF16), v) * (1.0 / total)
        for t in range(t0, t1):
            part = o[:, (t - t0) * LANES : (t - t0 + 1) * LANES]
            acc[t] = part if acc[t] is None else acc[t] + part
    for t in range(tiles):
        out[:, t * LANES : (t + 1) * LANES] = acc[t].astype(BF16)


def norm_kernel(core, hidden, attn_own, attn_other, w_own, w_other, out, half):
    mixed = (
        hidden[...].astype(F32)
        + dot_n(attn_own[...], w_own[...])
        + dot_n(attn_other[...], w_other[...])
    )
    mean = jnp.mean(mixed * mixed, axis=1, keepdims=True)
    out[...] = (mixed * lax.rsqrt(mean + 1e-05)).astype(BF16)
    n = half.shape[0]
    half[...] = out[pl.ds(pl.multiple_of(core[0] * n, n), n), :]


def stacked_queries(q, group, ratio):
    first = group * ratio * HEAD_SIZE
    return jnp.concatenate(
        [q[:, first + i * HEAD_SIZE : first + (i + 1) * HEAD_SIZE] for i in range(ratio)], axis=0
    )


def self_kernel(seq, q, own, back1, back2, out):
    rows = q.shape[0]
    groups = own.shape[1] // HEAD_SIZE
    ratio = q.shape[1] // HEAD_SIZE // groups
    scale = LOG2E / math.sqrt(HEAD_SIZE)
    blocks = (back2, back1, own)
    ids = [b[2 * rows : 2 * rows + ID_ROWS, 0:rows][0:1].astype(F32) for b in blocks]
    own_ids = column_of(ids[2])
    t = lax.broadcasted_iota(jnp.int32, (rows, rows), 0)
    k = lax.broadcasted_iota(jnp.int32, (rows, rows), 1)
    ok = [
        (ids[0] == own_ids) & (seq[0] >= 2),
        (ids[1] == own_ids) & (seq[0] >= 1),
        (ids[2] == own_ids) & (k <= t),
    ]
    bias = jnp.concatenate([jnp.where(m, 0.0, NEG) for m in ok], axis=1)
    bias = jnp.concatenate([bias] * ratio, axis=0)
    ones = jnp.ones((len(blocks) * rows, HEAD_SIZE), BF16)
    for g in range(groups):
        cols = slice(g * HEAD_SIZE, (g + 1) * HEAD_SIZE)
        keys = jnp.concatenate([b[0:rows, cols] for b in blocks], axis=0)
        values = jnp.concatenate([b[rows : 2 * rows, cols] for b in blocks], axis=0)
        s = dot_t(stacked_queries(q, g, ratio), keys) + bias
        p = jnp.exp2((s - jnp.max(s, axis=1, keepdims=True)) * scale).astype(BF16)
        o = dot_n(p, jnp.concatenate([values, ones], axis=1))
        o = o[:, :HEAD_SIZE] * (1.0 / o[:, HEAD_SIZE:])
        for i in range(ratio):
            j = g * ratio + i
            out[:, j * HEAD_SIZE : (j + 1) * HEAD_SIZE] = o[i * rows : (i + 1) * rows]


def cross_kernel(pieces, place, q, self_out, span, gate, norm_own, before_a, before_b, *refs):
    weights, out, w, kv = refs[:pieces], refs[pieces], refs[pieces + 1], refs[pieces + 2]
    rows = q.shape[0]
    tile = norm_own.shape[0]
    part = before_a.shape[0]
    kv_cols = w.shape[1] // 2
    groups = kv_cols // HEAD_SIZE
    ratio = q.shape[1] // HEAD_SIZE // groups
    scale = LOG2E / math.sqrt(HEAD_SIZE)
    for i, piece in enumerate(weights):
        n = piece.shape[0]
        start = place[2 + i]
        w[pl.ds(pl.multiple_of(start, ID_ROWS), n), :] = piece[...]
    before = jnp.concatenate([before_a[...], before_b[...]], axis=0)
    kv[0:tile, :] = dot_n(before, w[...]).astype(BF16)
    kv[tile : 2 * tile, :] = dot_n(norm_own[...], w[...]).astype(BF16)
    seq = place[0]
    low = column_of(span[0:1, :].astype(F32))
    high = column_of(span[1:2, :].astype(F32))
    this = seq.astype(F32)
    see_own = (low <= this) & (this < high)
    see_before = (low <= this - 1.0) & (this - 1.0 < high)
    see_own = jnp.concatenate([see_own.astype(F32)] * ratio, axis=0) > 0.5
    see_before = jnp.concatenate([see_before.astype(F32)] * ratio, axis=0) > 0.5
    ones = jnp.ones((tile, HEAD_SIZE), BF16)
    for g in range(groups):
        cols = slice(g * HEAD_SIZE, (g + 1) * HEAD_SIZE)
        vcols = slice(kv_cols + g * HEAD_SIZE, kv_cols + (g + 1) * HEAD_SIZE)
        queries = stacked_queries(q, g, ratio)
        s_before = dot_t(queries, kv[0:tile, cols])
        s_own = dot_t(queries, kv[tile : 2 * tile, cols])
        m = jnp.maximum(
            jnp.where(see_before, jnp.max(s_before, axis=1, keepdims=True), NEG),
            jnp.where(see_own, jnp.max(s_own, axis=1, keepdims=True), NEG),
        )
        p_before = jnp.exp2((s_before - jnp.where(see_before, m, -NEG)) * scale).astype(BF16)
        p_own = jnp.exp2((s_own - jnp.where(see_own, m, -NEG)) * scale).astype(BF16)
        o = dot_n(p_before, jnp.concatenate([kv[0:tile, vcols], ones], axis=1))
        o = o + dot_n(p_own, jnp.concatenate([kv[tile : 2 * tile, vcols], ones], axis=1))
        total = o[:, HEAD_SIZE:]
        o = o[:, :HEAD_SIZE] * jnp.where(total > 0.0, 1.0 / total, 0.0)
        for i in range(ratio):
            at = slice((g * ratio + i) * HEAD_SIZE, (g * ratio + i + 1) * HEAD_SIZE)
            out[:, at] = (self_out[:, at] + gate[:, at] * o[i * rows : (i + 1) * rows]).astype(BF16)


def shifted(block, axis, distance):
    n = lax.axis_size(axis)
    return lax.ppermute(block, axis, [(i, i + distance) for i in range(n - distance)])


def flipped(block, axis, bits):
    return lax.ppermute(block, axis, [(i, i ^ bits) for i in range(lax.axis_size(axis))])


def gathered_weights(w):
    n, rows = lax.axis_size("seq"), w.shape[0]
    me = lax.axis_index("seq")
    if n != 8 or lax.axis_size("groups") != 2 or rows % 32:
        return [(lax.all_gather(w, "seq", axis=0, tiled=True), 0)]
    group = lax.axis_index("groups")
    half = rows // 2
    mine, other = group * half, (1 - group) * half
    part = lax.dynamic_slice_in_dim(w, mine, half, 0)
    pieces = [(w, me * rows), (flipped(w, "seq", 1), (me ^ 1) * rows)]
    for z in (2, 4, 6):
        near = flipped(part, "seq", z)
        across = flipped(near, "seq", 1)
        pieces += [
            (near, (me ^ z) * rows + mine),
            (flipped(near, "groups", 1), (me ^ z) * rows + other),
            (across, (me ^ z ^ 1) * rows + mine),
            (flipped(across, "groups", 1), (me ^ z ^ 1) * rows + other),
        ]
    return pieces


def per_device(
    text_query_rows,
    text_key_value,
    doc_ids,
    tile_span,
    vision_hidden,
    vision_qkv,
    vision_out_weight,
    cross_keyvalue_weight,
    cross_gate,
):
    text_rows = text_query_rows.shape[0]
    tile_rows, width = vision_hidden.shape
    kv_cols = text_key_value.shape[2]
    kv_heads = kv_cols // HEAD_SIZE
    q_heads = text_query_rows.shape[1] // HEAD_SIZE
    seq = lax.axis_index("seq")
    core = lax.axis_index("head")
    other_core = functools.partial(flipped, axis="head", bits=1)
    sds = jax.ShapeDtypeStruct

    w = cross_keyvalue_weight.reshape(cross_keyvalue_weight.shape[0], -1)
    pieces = gathered_weights(w)
    out_weight_other = other_core(vision_out_weight)

    attn = call(
        vision_kernel,
        sds((tile_rows, vision_qkv.shape[2]), BF16),
        (vision_qkv,),
        flops=4 * tile_rows * tile_rows * vision_qkv.shape[2],
        transcendentals=tile_rows * tile_rows * vision_qkv.shape[2] // VHD,
    )
    attn_other = other_core(attn)
    norm, norm_half = call(
        norm_kernel,
        (sds((tile_rows, width), BF16), sds((tile_rows // 2, width), BF16)),
        (
            core.reshape(1),
            vision_hidden,
            attn,
            attn_other,
            vision_out_weight,
            out_weight_other,
        ),
        smem=1,
        flops=2 * tile_rows * width * width,
    )
    before_mine = shifted(norm_half, "seq", 1)
    before_other = other_core(before_mine)
    before_a = jnp.where(core == 0, before_mine, before_other)
    before_b = jnp.where(core == 0, before_other, before_mine)

    ids = jnp.broadcast_to(doc_ids.astype(BF16), (ID_ROWS, text_rows))
    ids = jnp.pad(ids, ((0, 0), (0, kv_cols - text_rows)))
    text = jnp.concatenate([text_key_value.reshape(-1, kv_cols), ids], axis=0)
    back1 = shifted(text, "seq", 1)
    back2 = shifted(text, "seq", 2)
    self_out = call(
        self_kernel,
        sds(text_query_rows.shape, F32),
        (seq.reshape(1), text_query_rows, text, back1, back2),
        smem=1,
        flops=4 * text_rows * q_heads * (WINDOW_BLOCKS + 1) * text_rows * HEAD_SIZE,
        transcendentals=text_rows * q_heads * (WINDOW_BLOCKS + 1) * text_rows,
    )

    gate = jnp.repeat(jnp.tanh(cross_gate), HEAD_SIZE)[None, :]
    place = jnp.stack([seq, core] + [jnp.asarray(p[1], jnp.int32) for p in pieces])
    return call(
        functools.partial(cross_kernel, len(pieces)),
        sds(text_query_rows.shape, BF16),
        (
            place,
            text_query_rows,
            self_out,
            tile_span.T,
            gate,
            norm,
            before_a,
            before_b,
            *[p[0] for p in pieces],
        ),
        smem=1,
        scratch=(
            pltpu.VMEM((width, 2 * kv_cols), BF16),
            pltpu.VMEM((2 * tile_rows, 2 * kv_cols), BF16),
        ),
        flops=4 * tile_rows * width * 2 * kv_cols
        + 4 * text_rows * q_heads * 2 * tile_rows * HEAD_SIZE,
        transcendentals=text_rows * q_heads * 2 * tile_rows,
    )


def solution(mesh):
    placed = (
        P(("groups", "seq"), "head"),
        P(None, ("groups", "seq"), "head"),
        P(("groups", "seq")),
        P(("groups", "seq"), None),
        P(("groups", "seq"), None),
        P(None, ("groups", "seq"), "head"),
        P("head", None),
        P("seq", None, "head"),
        P("head"),
    )
    return jax.shard_map(
        per_device,
        mesh=mesh,
        in_specs=placed,
        out_specs=P(("groups", "seq"), "head"),
        check_vma=False,
    )
```

```python
import functools
import math

import jax
import jax.numpy as jnp
from jax import lax
from jax.experimental import pallas as pl
from jax.experimental.pallas import tpu as pltpu
from jax.sharding import PartitionSpec as P

HEAD_SIZE = 128
VHD = 80
LANES = 128
WINDOW_BLOCKS = 2
ID_ROWS = 16
NEG = -1e30
LOG2E = math.log2(math.e)
F32 = jnp.float32
BF16 = jnp.bfloat16
PLANNED_FLOPS = 20_000_000_000
VMEM_LIMIT = 40 * 1024 * 1024


def dot_t(a, b):
    return lax.dot_general(a, b, (((1,), (1,)), ((), ())), preferred_element_type=F32)


def dot_n(a, b):
    return lax.dot_general(a, b, (((1,), (0,)), ((), ())), preferred_element_type=F32)


def column_of(row):
    n = row.shape[1]
    at = lax.broadcasted_iota(jnp.int32, (n, n), 0) == lax.broadcasted_iota(jnp.int32, (n, n), 1)
    return jnp.sum(jnp.where(at, row, 0.0), axis=1, keepdims=True)


def call(kernel, out_shape, args, smem=0, scratch=()):
    many = isinstance(out_shape, (tuple, list))
    vmem = pl.BlockSpec(memory_space=pltpu.VMEM)
    outs = out_shape if many else (out_shape,)
    moved = sum(math.prod(a.shape) * jnp.dtype(a.dtype).itemsize for a in (*args, *outs))
    return pl.pallas_call(
        kernel,
        out_shape=out_shape,
        in_specs=[pl.BlockSpec(memory_space=pltpu.SMEM)] * smem + [vmem] * (len(args) - smem),
        out_specs=[vmem] * len(out_shape) if many else vmem,
        scratch_shapes=list(scratch),
        compiler_params=pltpu.CompilerParams(vmem_limit_bytes=VMEM_LIMIT),
        cost_estimate=pl.CostEstimate(flops=PLANNED_FLOPS, bytes_accessed=moved, transcendentals=0),
    )(*args)


def vision_kernel(qkv, out):
    rows, cols = out.shape
    tiles = cols // LANES
    acc = [None] * tiles
    scale = LOG2E / math.sqrt(VHD)
    for head in range(cols // VHD):
        first, last = head * VHD, (head + 1) * VHD
        t0, t1 = first // LANES, -(-last // LANES)
        lanes = slice(t0 * LANES, t1 * LANES)
        lane = lax.broadcasted_iota(jnp.int32, (rows, (t1 - t0) * LANES), 1) + t0 * LANES
        mine = (lane >= first) & (lane < last)
        q = jnp.where(mine, qkv[0, :, lanes], jnp.zeros((), BF16))
        v = jnp.where(mine, qkv[2, :, lanes], jnp.zeros((), BF16))
        s = dot_t(q, qkv[1, :, lanes])
        p = jnp.exp2((s - jnp.max(s, axis=1, keepdims=True)) * scale)
        total = jnp.sum(p, axis=1, keepdims=True)
        o = dot_n(p.astype(BF16), v) * (1.0 / total)
        for t in range(t0, t1):
            part = o[:, (t - t0) * LANES : (t - t0 + 1) * LANES]
            acc[t] = part if acc[t] is None else acc[t] + part
    for t in range(tiles):
        out[:, t * LANES : (t + 1) * LANES] = acc[t].astype(BF16)


def rows_kernel(w, out):
    cols = w.shape[2]
    out[:, 0:cols] = w[:, 0, :]
    out[:, cols : 2 * cols] = w[:, 1, :]


def norm_kernel(core, hidden, attn_own, attn_other, w_own, w_other, out, half):
    mixed = (
        hidden[...].astype(F32)
        + dot_n(attn_own[...], w_own[...])
        + dot_n(attn_other[...], w_other[...])
    )
    mean = jnp.mean(mixed * mixed, axis=1, keepdims=True)
    out[...] = (mixed * lax.rsqrt(mean + 1e-05)).astype(BF16)
    n = half.shape[0]
    half[...] = out[pl.ds(pl.multiple_of(core[0] * n, n), n), :]


def stacked_queries(q, group, ratio):
    first = group * ratio * HEAD_SIZE
    return jnp.concatenate(
        [q[:, first + i * HEAD_SIZE : first + (i + 1) * HEAD_SIZE] for i in range(ratio)], axis=0
    )


def self_kernel(seq, q, own, back1, back2, out):
    rows = q.shape[0]
    groups = own.shape[1] // HEAD_SIZE
    ratio = q.shape[1] // HEAD_SIZE // groups
    scale = LOG2E / math.sqrt(HEAD_SIZE)
    blocks = (back2, back1, own)
    ids = [b[2 * rows : 2 * rows + ID_ROWS, 0:rows][0:1].astype(F32) for b in blocks]
    own_ids = column_of(ids[2])
    t = lax.broadcasted_iota(jnp.int32, (rows, rows), 0)
    k = lax.broadcasted_iota(jnp.int32, (rows, rows), 1)
    ok = [
        (ids[0] == own_ids) & (seq[0] >= 2),
        (ids[1] == own_ids) & (seq[0] >= 1),
        (ids[2] == own_ids) & (k <= t),
    ]
    bias = jnp.concatenate([jnp.where(m, 0.0, NEG) for m in ok], axis=1)
    bias = jnp.concatenate([bias] * ratio, axis=0)
    ones = jnp.ones((len(blocks) * rows, HEAD_SIZE), BF16)
    for g in range(groups):
        cols = slice(g * HEAD_SIZE, (g + 1) * HEAD_SIZE)
        keys = jnp.concatenate([b[0:rows, cols] for b in blocks], axis=0)
        values = jnp.concatenate([b[rows : 2 * rows, cols] for b in blocks], axis=0)
        s = dot_t(stacked_queries(q, g, ratio), keys) + bias
        p = jnp.exp2((s - jnp.max(s, axis=1, keepdims=True)) * scale).astype(BF16)
        o = dot_n(p, jnp.concatenate([values, ones], axis=1))
        o = o[:, :HEAD_SIZE] * (1.0 / o[:, HEAD_SIZE:])
        for i in range(ratio):
            j = g * ratio + i
            out[:, j * HEAD_SIZE : (j + 1) * HEAD_SIZE] = o[i * rows : (i + 1) * rows]


def cross_kernel(pieces, place, q, self_out, span, gate, norm_own, before_a, before_b, *refs):
    weights, out, w, kv = refs[:pieces], refs[pieces], refs[pieces + 1], refs[pieces + 2]
    rows = q.shape[0]
    tile = norm_own.shape[0]
    kv_cols = w.shape[1] // 2
    groups = kv_cols // HEAD_SIZE
    ratio = q.shape[1] // HEAD_SIZE // groups
    scale = LOG2E / math.sqrt(HEAD_SIZE)
    for i, piece in enumerate(weights):
        n = piece.shape[0]
        start = place[2 + i]
        w[pl.ds(pl.multiple_of(start, ID_ROWS), n), :] = piece[...]
    norms = jnp.concatenate([before_a[...], before_b[...], norm_own[...]], axis=0)
    kv[...] = dot_n(norms, w[...]).astype(BF16)
    this = place[0].astype(F32)
    low = column_of(span[0:1, :].astype(F32))
    high = column_of(span[1:2, :].astype(F32))
    see_own = (low <= this) & (this < high)
    see_before = (low <= this - 1.0) & (this - 1.0 < high)
    present = jnp.broadcast_to(jnp.where(low < high, 1.0, 0.0), (rows, HEAD_SIZE))
    bias = jnp.concatenate(
        [
            jnp.broadcast_to(jnp.where(see, 0.0, NEG), (rows, tile))
            for see in (see_before, see_own)
        ],
        axis=1,
    )
    ones = jnp.ones((2 * tile, HEAD_SIZE), BF16)
    for g in range(groups):
        keys = kv[:, g * HEAD_SIZE : (g + 1) * HEAD_SIZE]
        values = kv[:, kv_cols + g * HEAD_SIZE : kv_cols + (g + 1) * HEAD_SIZE]
        values = jnp.concatenate([values, ones], axis=1)
        for i in range(ratio):
            at = slice((g * ratio + i) * HEAD_SIZE, (g * ratio + i + 1) * HEAD_SIZE)
            s = dot_t(q[:, at], keys) + bias
            p = jnp.exp2((s - jnp.max(s, axis=1, keepdims=True)) * scale).astype(BF16)
            o = dot_n(p, values)
            o = o[:, :HEAD_SIZE] * (1.0 / o[:, HEAD_SIZE:])
            out[:, at] = (self_out[:, at] + gate[:, at] * present * o).astype(BF16)


def mark_kernel(x, out):
    out[...] = x[...]


def marker(*done):
    x = after(jnp.zeros((8, LANES), F32), *done)
    return call(mark_kernel, jax.ShapeDtypeStruct(x.shape, F32), (x,))


def shifted(block, axis, distance):
    n = lax.axis_size(axis)
    return lax.ppermute(block, axis, [(i, i + distance) for i in range(n - distance)])


def flipped(block, axis, bits):
    return lax.ppermute(block, axis, [(i, i ^ bits) for i in range(lax.axis_size(axis))])


def after(x, *done):
    return lax.optimization_barrier((x, *done))[0]


def per_device(
    text_query_rows,
    text_key_value,
    doc_ids,
    tile_span,
    vision_hidden,
    vision_qkv,
    vision_out_weight,
    cross_keyvalue_weight,
    cross_gate,
):
    text_rows = text_query_rows.shape[0]
    tile_rows, width = vision_hidden.shape
    kv_cols = text_key_value.shape[2]
    kv_heads = kv_cols // HEAD_SIZE
    q_heads = text_query_rows.shape[1] // HEAD_SIZE
    seq = lax.axis_index("seq")
    core = lax.axis_index("head")
    other_core = functools.partial(flipped, axis="head", bits=1)
    sds = jax.ShapeDtypeStruct

    rows = cross_keyvalue_weight.shape[0]
    n = lax.axis_size("seq")
    half = rows // 2
    ring = [i for i in range(0, n, 2)] + [i for i in range(n - 1, 0, -2)]
    rings = n == 8 and rows % 32 == 0
    even = seq % 2 == 0

    def around(blocks):
        if not rings:
            return ()
        up, down = blocks
        return (
            lax.ppermute(up, "seq", [(ring[i - 1], ring[i]) for i in range(n)]),
            lax.ppermute(down, "seq", [(ring[i], ring[i - 1]) for i in range(n)]),
        )

    (w,) = call(
        rows_kernel,
        (sds((rows, 2 * kv_cols), BF16),),
        (cross_keyvalue_weight,),
    )
    out_weight_other = other_core(vision_out_weight)
    ids = jnp.broadcast_to(doc_ids.astype(BF16), (ID_ROWS, text_rows))
    ids = jnp.pad(ids, ((0, 0), (0, kv_cols - text_rows)))
    text = jnp.concatenate([text_key_value.reshape(-1, kv_cols), ids], axis=0)
    step1 = around((w, w))
    attn = call(
        vision_kernel,
        sds((tile_rows, vision_qkv.shape[2]), BF16),
        (after(vision_qkv, w),),
    )
    attn_other = other_core(attn)
    back2 = shifted(after(text, attn), "seq", 2)
    mark = marker(attn)
    step2 = around([after(block, mark) for block in step1])
    norm, norm_half = call(
        norm_kernel,
        (sds((tile_rows, width), BF16), sds((tile_rows // 2, width), BF16)),
        (
            core.reshape(1),
            after(vision_hidden, back2, *step1),
            attn,
            attn_other,
            vision_out_weight,
            out_weight_other,
        ),
        smem=1,
    )
    mark = marker(norm)
    step3 = around([after(block, mark) for block in step2])
    back1 = flipped(after(jnp.where(even, text, back2), norm), "seq", 1)
    before_mine = shifted(norm_half, "seq", 1)
    before_other = other_core(before_mine)
    before_a = jnp.where(core == 0, before_mine, before_other)
    before_b = jnp.where(core == 0, before_other, before_mine)
    self_out = call(
        self_kernel,
        sds(text_query_rows.shape, F32),
        (seq.reshape(1), after(text_query_rows, before_mine), text, back1, back2),
        smem=1,
    )
    if rings:
        up, down = [after(block, self_out) for block in step3]
        step4 = around((up[:half], down[half:]))
        at = lambda p: jnp.where(p % n < n // 2, 2 * (p % n), 2 * (n - 1 - p % n) + 1) * rows
        place = jnp.where(even, seq // 2, n - 1 - seq // 2)
        pieces = [(w, seq * rows)]
        for k, (up, down) in ((1, step1), (2, step2), (3, step3)):
            pieces += [(up, at(place + n - k)), (down, at(place + k))]
        pieces += [(step4[0], at(place + n // 2)), (step4[1], at(place + n // 2) + half)]
    else:
        pieces = [(lax.all_gather(w, "seq", axis=0, tiled=True), 0)]

    gate = jnp.repeat(jnp.tanh(cross_gate), HEAD_SIZE)[None, :]
    place = jnp.stack([seq, core] + [jnp.asarray(p[1], jnp.int32) for p in pieces])
    return call(
        functools.partial(cross_kernel, len(pieces)),
        sds(text_query_rows.shape, BF16),
        (
            place,
            text_query_rows,
            self_out,
            tile_span.T,
            gate,
            norm,
            before_a,
            before_b,
            *[p[0] for p in pieces],
        ),
        smem=1,
        scratch=(
            pltpu.VMEM((width, 2 * kv_cols), BF16),
            pltpu.VMEM((2 * tile_rows, 2 * kv_cols), BF16),
        ),
    )


def solution(mesh):
    placed = (
        P(("groups", "seq"), "head"),
        P(None, ("groups", "seq"), "head"),
        P(("groups", "seq")),
        P(("groups", "seq"), None),
        P(("groups", "seq"), None),
        P(None, ("groups", "seq"), "head"),
        P("head", None),
        P("seq", None, "head"),
        P("head"),
    )
    return jax.shard_map(
        per_device,
        mesh=mesh,
        in_specs=placed,
        out_specs=P(("groups", "seq"), "head"),
        check_vma=False,
    )
```

```python
import functools
import math

import jax
import jax.numpy as jnp
from jax import lax
from jax.experimental import pallas as pl
from jax.experimental.pallas import tpu as pltpu
from jax.sharding import PartitionSpec as P

HEAD_SIZE = 128
VHD = 80
LANES = 128
WINDOW_BLOCKS = 2
ID_ROWS = 16
NEG = -1e30
LOG2E = math.log2(math.e)
F32 = jnp.float32
BF16 = jnp.bfloat16
PLANNED_FLOPS = 20000000000
VMEM_LIMIT = 40 * 1024 * 1024


def dot_t(a, b):
    return lax.dot_general(a, b, (((1,), (1,)), ((), ())), preferred_element_type=F32)


def dot_n(a, b):
    return lax.dot_general(a, b, (((1,), (0,)), ((), ())), preferred_element_type=F32)


def column_of(row):
    n = row.shape[1]
    at = lax.broadcasted_iota(jnp.int32, (n, n), 0) == lax.broadcasted_iota(jnp.int32, (n, n), 1)
    return jnp.sum(jnp.where(at, row, 0.0), axis=1, keepdims=True)


def call(kernel, out_shape, args, smem=0, scratch=()):
    many = isinstance(out_shape, (tuple, list))
    vmem = pl.BlockSpec(memory_space=pltpu.VMEM)
    outs = out_shape if many else (out_shape,)
    moved = sum(math.prod(a.shape) * jnp.dtype(a.dtype).itemsize for a in (*args, *outs))
    return pl.pallas_call(
        kernel,
        out_shape=out_shape,
        in_specs=[pl.BlockSpec(memory_space=pltpu.SMEM)] * smem + [vmem] * (len(args) - smem),
        out_specs=[vmem] * len(out_shape) if many else vmem,
        scratch_shapes=list(scratch),
        compiler_params=pltpu.CompilerParams(vmem_limit_bytes=VMEM_LIMIT),
        cost_estimate=pl.CostEstimate(flops=PLANNED_FLOPS, bytes_accessed=moved, transcendentals=0),
    )(*args)


def vision_kernel(qkv, out):
    rows, cols = out.shape
    tiles = cols // LANES
    acc = [None] * tiles
    scale = LOG2E / math.sqrt(VHD)
    for head in range(cols // VHD):
        first, last = head * VHD, (head + 1) * VHD
        t0, t1 = first // LANES, -(-last // LANES)
        lanes = slice(t0 * LANES, t1 * LANES)
        lane = lax.broadcasted_iota(jnp.int32, (rows, (t1 - t0) * LANES), 1) + t0 * LANES
        mine = (lane >= first) & (lane < last)
        q = jnp.where(mine, qkv[0, :, lanes], jnp.zeros((), BF16))
        v = jnp.where(mine, qkv[2, :, lanes], jnp.zeros((), BF16))
        s = dot_t(q, qkv[1, :, lanes])
        p = jnp.exp2((s - jnp.max(s, axis=1, keepdims=True)) * scale)
        total = jnp.sum(p, axis=1, keepdims=True)
        o = dot_n(p.astype(BF16), v) * (1.0 / total)
        for t in range(t0, t1):
            part = o[:, (t - t0) * LANES : (t - t0 + 1) * LANES]
            acc[t] = part if acc[t] is None else acc[t] + part
    for t in range(tiles):
        out[:, t * LANES : (t + 1) * LANES] = acc[t].astype(BF16)


def rows_kernel(w, out):
    cols = w.shape[2]
    out[:, 0:cols] = w[:, 0, :]
    out[:, cols : 2 * cols] = w[:, 1, :]


def norm_kernel(core, hidden, attn_own, attn_other, w_own, w_other, out, half):
    mixed = (
        hidden[...].astype(F32)
        + dot_n(attn_own[...], w_own[...])
        + dot_n(attn_other[...], w_other[...])
    )
    mean = jnp.mean(mixed * mixed, axis=1, keepdims=True)
    out[...] = (mixed * lax.rsqrt(mean + 1e-05)).astype(BF16)
    n = half.shape[0]
    half[...] = out[pl.ds(pl.multiple_of(core[0] * n, n), n), :]


def stacked_queries(q, group, ratio):
    first = group * ratio * HEAD_SIZE
    return jnp.concatenate(
        [q[:, first + i * HEAD_SIZE : first + (i + 1) * HEAD_SIZE] for i in range(ratio)], axis=0
    )


def self_kernel(seq, q, own, back1, back2, out):
    rows = q.shape[0]
    groups = own.shape[1] // HEAD_SIZE
    ratio = q.shape[1] // HEAD_SIZE // groups
    scale = LOG2E / math.sqrt(HEAD_SIZE)
    blocks = (back2, back1, own)
    ids = [b[2 * rows : 2 * rows + ID_ROWS, 0:rows][0:1].astype(F32) for b in blocks]
    own_ids = column_of(ids[2])
    t = lax.broadcasted_iota(jnp.int32, (rows, rows), 0)
    k = lax.broadcasted_iota(jnp.int32, (rows, rows), 1)
    ok = [
        (ids[0] == own_ids) & (seq[0] >= 2),
        (ids[1] == own_ids) & (seq[0] >= 1),
        (ids[2] == own_ids) & (k <= t),
    ]
    bias = jnp.concatenate([jnp.where(m, 0.0, NEG) for m in ok], axis=1)
    bias = jnp.concatenate([bias] * ratio, axis=0)
    ones = jnp.ones((len(blocks) * rows, HEAD_SIZE), BF16)
    for g in range(groups):
        cols = slice(g * HEAD_SIZE, (g + 1) * HEAD_SIZE)
        keys = jnp.concatenate([b[0:rows, cols] for b in blocks], axis=0)
        values = jnp.concatenate([b[rows : 2 * rows, cols] for b in blocks], axis=0)
        s = dot_t(stacked_queries(q, g, ratio), keys) + bias
        p = jnp.exp2((s - jnp.max(s, axis=1, keepdims=True)) * scale).astype(BF16)
        o = dot_n(p, jnp.concatenate([values, ones], axis=1))
        o = o[:, :HEAD_SIZE] * (1.0 / o[:, HEAD_SIZE:])
        for i in range(ratio):
            j = g * ratio + i
            out[:, j * HEAD_SIZE : (j + 1) * HEAD_SIZE] = o[i * rows : (i + 1) * rows]


def cross_kernel(pieces, place, q, self_out, span, gate, norm_own, before_mine, before_other, *refs):
    weights, out, w, kv = refs[:pieces], refs[pieces], refs[pieces + 1], refs[pieces + 2]
    rows = q.shape[0]
    tile = norm_own.shape[0]
    kv_cols = w.shape[1] // 2
    groups = kv_cols // HEAD_SIZE
    ratio = q.shape[1] // HEAD_SIZE // groups
    scale = LOG2E / math.sqrt(HEAD_SIZE)
    for i, piece in enumerate(weights):
        n = piece.shape[0]
        start = place[2 + i]
        w[pl.ds(pl.multiple_of(start, ID_ROWS), n), :] = piece[...]
    first, mine, other = place[1] == 0, before_mine[...], before_other[...]
    norms = [jnp.where(first, mine, other), jnp.where(first, other, mine), norm_own[...]]
    norms = jnp.concatenate(norms, axis=0)
    kv[...] = dot_n(norms, w[...]).astype(BF16)
    this = place[0].astype(F32)
    low = column_of(span[0:1, :].astype(F32))
    high = column_of(span[1:2, :].astype(F32))
    see_own = (low <= this) & (this < high)
    see_before = (low <= this - 1.0) & (this - 1.0 < high)
    present = jnp.broadcast_to(jnp.where(low < high, 1.0, 0.0), (rows, HEAD_SIZE))
    bias = jnp.concatenate(
        [
            jnp.broadcast_to(jnp.where(see, 0.0, NEG), (rows, tile))
            for see in (see_before, see_own)
        ],
        axis=1,
    )
    ones = jnp.ones((2 * tile, HEAD_SIZE), BF16)
    for g in range(groups):
        keys = kv[:, g * HEAD_SIZE : (g + 1) * HEAD_SIZE]
        values = kv[:, kv_cols + g * HEAD_SIZE : kv_cols + (g + 1) * HEAD_SIZE]
        values = jnp.concatenate([values, ones], axis=1)
        for i in range(ratio):
            at = slice((g * ratio + i) * HEAD_SIZE, (g * ratio + i + 1) * HEAD_SIZE)
            s = dot_t(q[:, at], keys) + bias
            p = jnp.exp2((s - jnp.max(s, axis=1, keepdims=True)) * scale).astype(BF16)
            o = dot_n(p, values)
            o = o[:, :HEAD_SIZE] * (1.0 / o[:, HEAD_SIZE:])
            out[:, at] = (self_out[:, at] + gate[:, at] * present * o).astype(BF16)


def mark_kernel(x, out):
    out[...] = x[...]


def marker(*done):
    x = after(jnp.zeros((8, LANES), F32), *done)
    return call(mark_kernel, jax.ShapeDtypeStruct(x.shape, F32), (x,))


def shifted(block, axis, distance):
    n = lax.axis_size(axis)
    return lax.ppermute(block, axis, [(i, i + distance) for i in range(n - distance)])


def flipped(block, axis, bits):
    return lax.ppermute(block, axis, [(i, i ^ bits) for i in range(lax.axis_size(axis))])


def after(x, *done):
    return lax.optimization_barrier((x, *done))[0]


def per_device(
    text_query_rows,
    text_key_value,
    doc_ids,
    tile_span,
    vision_hidden,
    vision_qkv,
    vision_out_weight,
    cross_keyvalue_weight,
    cross_gate,
):
    text_rows = text_query_rows.shape[0]
    tile_rows, width = vision_hidden.shape
    kv_cols = text_key_value.shape[2]
    kv_heads = kv_cols // HEAD_SIZE
    q_heads = text_query_rows.shape[1] // HEAD_SIZE
    seq = lax.axis_index("seq")
    core = lax.axis_index("head")
    other_core = functools.partial(flipped, axis="head", bits=1)
    sds = jax.ShapeDtypeStruct

    rows = cross_keyvalue_weight.shape[0]
    n = lax.axis_size("seq")
    half = rows // 2
    ring = [i for i in range(0, n, 2)] + [i for i in range(n - 1, 0, -2)]
    rings = n == 8 and rows % 32 == 0
    even = seq % 2 == 0

    chunks = 1
    ways = [(ring[i - 1], ring[i]) for i in range(n)], [(ring[i], ring[i - 1]) for i in range(n)]

    def around(blocks):
        return [lax.ppermute(block, "seq", ways[way]) for way, block in blocks] if rings else []

    ids = jnp.broadcast_to(doc_ids.astype(BF16), (ID_ROWS, text_rows))
    ids = jnp.pad(ids, ((0, 0), (0, kv_cols - text_rows)))
    text = jnp.concatenate([text_key_value.reshape(-1, kv_cols), ids], axis=0)
    (w,) = call(
        rows_kernel,
        (sds((rows, 2 * kv_cols), BF16),),
        (cross_keyvalue_weight,),
    )
    out_weight_other = other_core(vision_out_weight)
    step1 = around([(way, w[c * rows // chunks : (c + 1) * rows // chunks]) for c in range(chunks) for way in (0, 1)])
    attn = call(
        vision_kernel,
        sds((tile_rows, vision_qkv.shape[2]), BF16),
        (vision_qkv,),
    )
    attn_other = other_core(attn)
    back2 = shifted(text, "seq", 2)
    step2 = around([(i % 2, block) for i, block in enumerate(step1)])
    norm, norm_half = call(
        norm_kernel,
        (sds((tile_rows, width), BF16), sds((tile_rows // 2, width), BF16)),
        (
            core.reshape(1),
            vision_hidden,
            attn,
            attn_other,
            vision_out_weight,
            out_weight_other,
        ),
        smem=1,
    )
    step3 = around([(i % 2, block) for i, block in enumerate(step2)])
    back1 = flipped(jnp.where(even, text, back2), "seq", 1)
    before_mine = shifted(norm_half, "seq", 1)
    before_other = other_core(before_mine)
    self_out = call(
        self_kernel,
        sds(text_query_rows.shape, F32),
        (seq.reshape(1), text_query_rows, text, back1, back2),
        smem=1,
    )
    if rings:
        up, down = [block for block in (step3[0], step3[-1])]
        step4 = around([(0, up[:half]), (1, down[-half:])])
    if rings:
        at = lambda p: jnp.where(p % n < n // 2, 2 * (p % n), 2 * (n - 1 - p % n) + 1) * rows
        place = jnp.where(even, seq // 2, n - 1 - seq // 2)
        pieces = [(w, seq * rows)]
        for k, step in ((1, step1), (2, step2), (3, step3)):
            for i, block in enumerate(step):
                first = at(place + (k if i % 2 else n - k)) + i // 2 * (rows // chunks)
                pieces += [(block, first)]
        pieces += [(step4[0], at(place + n // 2)), (step4[1], at(place + n // 2) + half)]
    else:
        pieces = [(lax.all_gather(w, "seq", axis=0, tiled=True), 0)]

    gate = jnp.repeat(jnp.tanh(cross_gate), HEAD_SIZE)[None, :]
    place = jnp.stack([seq, core] + [jnp.asarray(p[1], jnp.int32) for p in pieces])
    return call(
        functools.partial(cross_kernel, len(pieces)),
        sds(text_query_rows.shape, BF16),
        (
            place,
            text_query_rows,
            self_out,
            tile_span.T,
            gate,
            norm,
            before_mine,
            before_other,
            *[p[0] for p in pieces],
        ),
        smem=1,
        scratch=(
            pltpu.VMEM((width, 2 * kv_cols), BF16),
            pltpu.VMEM((2 * tile_rows, 2 * kv_cols), BF16),
        ),
    )


def solution(mesh):
    placed = (
        P(("groups", "seq"), "head"),
        P(None, ("groups", "seq"), "head"),
        P(("groups", "seq")),
        P(("groups", "seq"), None),
        P(("groups", "seq"), None),
        P(None, ("groups", "seq"), "head"),
        P("head", None),
        P("seq", None, "head"),
        P("head"),
    )
    return jax.shard_map(
        per_device,
        mesh=mesh,
        in_specs=placed,
        out_specs=P(("groups", "seq"), "head"),
        check_vma=False,
    )
```

```python
import functools
import math

import jax
import jax.numpy as jnp
from jax import lax
from jax.experimental import pallas as pl
from jax.experimental.pallas import tpu as pltpu
from jax.sharding import PartitionSpec as P

HEAD_SIZE = 128
VHD = 80
LANES = 128
WINDOW_BLOCKS = 2
ID_ROWS = 16
NEG = -1e30
LOG2E = math.log2(math.e)
F32 = jnp.float32
BF16 = jnp.bfloat16
PLANNED_FLOPS = 20000000000
VMEM_LIMIT = 40 * 1024 * 1024


def dot_t(a, b):
    return lax.dot_general(a, b, (((1,), (1,)), ((), ())), preferred_element_type=F32)


def dot_n(a, b):
    return lax.dot_general(a, b, (((1,), (0,)), ((), ())), preferred_element_type=F32)


def column_of(row):
    n = row.shape[1]
    at = lax.broadcasted_iota(jnp.int32, (n, n), 0) == lax.broadcasted_iota(jnp.int32, (n, n), 1)
    return jnp.sum(jnp.where(at, row, 0.0), axis=1, keepdims=True)


def call(kernel, out_shape, args, smem=0, hbm=0, scratch=()):
    many = isinstance(out_shape, (tuple, list))
    vmem = pl.BlockSpec(memory_space=pltpu.VMEM)
    anywhere = pl.BlockSpec(memory_space=pl.ANY)
    outs = out_shape if many else (out_shape,)
    moved = sum(math.prod(a.shape) * jnp.dtype(a.dtype).itemsize for a in (*args, *outs))
    return pl.pallas_call(
        kernel,
        out_shape=out_shape,
        in_specs=[pl.BlockSpec(memory_space=pltpu.SMEM)] * smem + [anywhere] * hbm
        + [vmem] * (len(args) - smem - hbm),
        out_specs=[vmem] * len(out_shape) if many else anywhere if hbm else vmem,
        scratch_shapes=list(scratch),
        compiler_params=pltpu.CompilerParams(vmem_limit_bytes=VMEM_LIMIT),
        cost_estimate=pl.CostEstimate(flops=PLANNED_FLOPS, bytes_accessed=moved, transcendentals=0),
    )(*args)


def vision_kernel(qkv, out):
    rows, cols = out.shape
    tiles = cols // LANES
    acc = [None] * tiles
    scale = LOG2E / math.sqrt(VHD)
    for head in range(cols // VHD):
        first, last = head * VHD, (head + 1) * VHD
        t0, t1 = first // LANES, -(-last // LANES)
        lanes = slice(t0 * LANES, t1 * LANES)
        lane = lax.broadcasted_iota(jnp.int32, (rows, (t1 - t0) * LANES), 1) + t0 * LANES
        mine = (lane >= first) & (lane < last)
        q = jnp.where(mine, qkv[0, :, lanes], jnp.zeros((), BF16))
        v = jnp.where(mine, qkv[2, :, lanes], jnp.zeros((), BF16))
        s = dot_t(q, qkv[1, :, lanes])
        p = jnp.exp2((s - jnp.max(s, axis=1, keepdims=True)) * scale)
        total = jnp.sum(p, axis=1, keepdims=True)
        o = dot_n(p.astype(BF16), v) * (1.0 / total)
        for t in range(t0, t1):
            part = o[:, (t - t0) * LANES : (t - t0 + 1) * LANES]
            acc[t] = part if acc[t] is None else acc[t] + part
    for t in range(tiles):
        out[:, t * LANES : (t + 1) * LANES] = acc[t].astype(BF16)


def rows_kernel(w, out):
    cols = w.shape[2]
    out[:, 0:cols] = w[:, 0, :]
    out[:, cols : 2 * cols] = w[:, 1, :]


def norm_kernel(core, hidden, attn_own, attn_other, w_own, w_other, out, half):
    mixed = (
        hidden[...].astype(F32)
        + dot_n(attn_own[...], w_own[...])
        + dot_n(attn_other[...], w_other[...])
    )
    mean = jnp.mean(mixed * mixed, axis=1, keepdims=True)
    out[...] = (mixed * lax.rsqrt(mean + 1e-05)).astype(BF16)
    n = half.shape[0]
    half[...] = out[pl.ds(pl.multiple_of(core[0] * n, n), n), :]


def stacked_queries(q, group, ratio):
    first = group * ratio * HEAD_SIZE
    return jnp.concatenate(
        [q[:, first + i * HEAD_SIZE : first + (i + 1) * HEAD_SIZE] for i in range(ratio)], axis=0
    )


def self_kernel(seq, q, own, back1, back2, out):
    rows = q.shape[0]
    groups = own.shape[1] // HEAD_SIZE
    ratio = q.shape[1] // HEAD_SIZE // groups
    scale = LOG2E / math.sqrt(HEAD_SIZE)
    blocks = (back2, back1, own)
    ids = [b[2 * rows : 2 * rows + ID_ROWS, 0:rows][0:1].astype(F32) for b in blocks]
    own_ids = column_of(ids[2])
    t = lax.broadcasted_iota(jnp.int32, (rows, rows), 0)
    k = lax.broadcasted_iota(jnp.int32, (rows, rows), 1)
    ok = [
        (ids[0] == own_ids) & (seq[0] >= 2),
        (ids[1] == own_ids) & (seq[0] >= 1),
        (ids[2] == own_ids) & (k <= t),
    ]
    bias = jnp.concatenate([jnp.where(m, 0.0, NEG) for m in ok], axis=1)
    bias = jnp.concatenate([bias] * ratio, axis=0)
    ones = jnp.ones((len(blocks) * rows, HEAD_SIZE), BF16)
    for g in range(groups):
        cols = slice(g * HEAD_SIZE, (g + 1) * HEAD_SIZE)
        keys = jnp.concatenate([b[0:rows, cols] for b in blocks], axis=0)
        values = jnp.concatenate([b[rows : 2 * rows, cols] for b in blocks], axis=0)
        s = dot_t(stacked_queries(q, g, ratio), keys) + bias
        p = jnp.exp2((s - jnp.max(s, axis=1, keepdims=True)) * scale).astype(BF16)
        o = dot_n(p, jnp.concatenate([values, ones], axis=1))
        o = o[:, :HEAD_SIZE] * (1.0 / o[:, HEAD_SIZE:])
        for i in range(ratio):
            j = g * ratio + i
            out[:, j * HEAD_SIZE : (j + 1) * HEAD_SIZE] = o[i * rows : (i + 1) * rows]


def image_kernel(pieces, late, place, norm_own, before_mine, before_other, *refs):
    weights, refs = refs[:pieces], refs[pieces:]
    total, w = refs[0], refs[-1]
    for i, piece in enumerate(weights):
        n = piece.shape[0]
        w[pl.ds(pl.multiple_of(place[3 + i], ID_ROWS), n), :] = piece[...]
    first, mine, other = place[1] == 0, before_mine[...], before_other[...]
    norms = [jnp.where(first, mine, other), jnp.where(first, other, mine), norm_own[...]]
    norms = jnp.concatenate(norms, axis=0)
    if late:
        w[pl.ds(pl.multiple_of(place[2], ID_ROWS), late), :] = jnp.zeros((late, w.shape[1]), BF16)
        shape = (w.shape[0], late)
        picks = lax.broadcasted_iota(jnp.int32, shape, 0) == (
            lax.broadcasted_iota(jnp.int32, shape, 1) + place[2]
        )
        refs[1][...] = dot_n(norms, jnp.where(picks, 1.0, 0.0).astype(BF16)).astype(BF16)
    total[...] = dot_n(norms, w[...])


def cross_kernel(seq, q_all, self_all, span, gate, total, *refs):
    late, (out_all, kv, q, self_out, out, sems) = refs[:-6], refs[-6:]
    rows = q.shape[0]
    tile = total.shape[0] // 2
    kv_cols = total.shape[1] // 2
    groups = kv_cols // HEAD_SIZE
    ratio = q.shape[1] // HEAD_SIZE // groups
    scale = LOG2E / math.sqrt(HEAD_SIZE)
    fetch_q = pltpu.make_async_copy(q_all, q, sems.at[0])
    fetch_self = pltpu.make_async_copy(self_all, self_out, sems.at[1])
    fetch_q.start()
    fetch_self.start()
    if late:
        rest = jnp.concatenate([block[...] for block in late[1:]], axis=0)
        kv[...] = (total[...] + dot_n(late[0][...], rest)).astype(BF16)
    else:
        kv[...] = total[...].astype(BF16)
    this = seq[0].astype(F32)
    low = column_of(span[0:1, :].astype(F32))
    high = column_of(span[1:2, :].astype(F32))
    see_own = (low <= this) & (this < high)
    see_before = (low <= this - 1.0) & (this - 1.0 < high)
    present = jnp.broadcast_to(jnp.where(low < high, 1.0, 0.0), (rows, HEAD_SIZE))
    bias = jnp.concatenate(
        [
            jnp.broadcast_to(jnp.where(see, 0.0, NEG), (rows, tile))
            for see in (see_before, see_own)
        ],
        axis=1,
    )
    ones = jnp.ones((2 * tile, HEAD_SIZE), BF16)
    fetch_q.wait()
    fetch_self.wait()
    stores = []
    for g in range(groups):
        keys = kv[:, g * HEAD_SIZE : (g + 1) * HEAD_SIZE]
        values = kv[:, kv_cols + g * HEAD_SIZE : kv_cols + (g + 1) * HEAD_SIZE]
        values = jnp.concatenate([values, ones], axis=1)
        for i in range(ratio):
            at = slice((g * ratio + i) * HEAD_SIZE, (g * ratio + i + 1) * HEAD_SIZE)
            s = dot_t(q[:, at], keys) + bias
            p = jnp.exp2((s - jnp.max(s, axis=1, keepdims=True)) * scale).astype(BF16)
            o = dot_n(p, values)
            o = o[:, :HEAD_SIZE] * (1.0 / o[:, HEAD_SIZE:])
            out[:, at] = (self_out[:, at] + gate[:, at] * present * o).astype(BF16)
        whole = slice(g * ratio * HEAD_SIZE, (g + 1) * ratio * HEAD_SIZE)
        stores.append(pltpu.make_async_copy(out.at[:, whole], out_all.at[:, whole], sems.at[2 + g]))
        stores[-1].start()
    for store in stores:
        store.wait()


def shifted(block, axis, distance):
    n = lax.axis_size(axis)
    return lax.ppermute(block, axis, [(i, i + distance) for i in range(n - distance)])


def flipped(block, axis, bits):
    return lax.ppermute(block, axis, [(i, i ^ bits) for i in range(lax.axis_size(axis))])


def per_device(
    text_query_rows,
    text_key_value,
    doc_ids,
    tile_span,
    vision_hidden,
    vision_qkv,
    vision_out_weight,
    cross_keyvalue_weight,
    cross_gate,
):
    text_rows = text_query_rows.shape[0]
    tile_rows, width = vision_hidden.shape
    kv_cols = text_key_value.shape[2]
    kv_heads = kv_cols // HEAD_SIZE
    q_heads = text_query_rows.shape[1] // HEAD_SIZE
    seq = lax.axis_index("seq")
    core = lax.axis_index("head")
    other_core = functools.partial(flipped, axis="head", bits=1)
    sds = jax.ShapeDtypeStruct

    rows = cross_keyvalue_weight.shape[0]
    n = lax.axis_size("seq")
    half = rows // 2
    ring = [i for i in range(0, n, 2)] + [i for i in range(n - 1, 0, -2)]
    rings = n == 8 and rows % 32 == 0
    even = seq % 2 == 0

    chunks = 1
    ways = [(ring[i - 1], ring[i]) for i in range(n)], [(ring[i], ring[i - 1]) for i in range(n)]

    def around(blocks):
        return [lax.ppermute(block, "seq", ways[way]) for way, block in blocks] if rings else []

    ids = jnp.broadcast_to(doc_ids.astype(BF16), (ID_ROWS, text_rows))
    ids = jnp.pad(ids, ((0, 0), (0, kv_cols - text_rows)))
    text = jnp.concatenate([text_key_value.reshape(-1, kv_cols), ids], axis=0)
    (w,) = call(
        rows_kernel,
        (sds((rows, 2 * kv_cols), BF16),),
        (cross_keyvalue_weight,),
    )
    out_weight_other = other_core(vision_out_weight)
    step1 = around([(way, w[c * rows // chunks : (c + 1) * rows // chunks]) for c in range(chunks) for way in (0, 1)])
    attn = call(
        vision_kernel,
        sds((tile_rows, vision_qkv.shape[2]), BF16),
        (vision_qkv,),
    )
    attn_other = other_core(attn)
    back2 = shifted(text, "seq", 2)
    step2 = around([(i % 2, block) for i, block in enumerate(step1)])
    norm, norm_half = call(
        norm_kernel,
        (sds((tile_rows, width), BF16), sds((tile_rows // 2, width), BF16)),
        (
            core.reshape(1),
            vision_hidden,
            attn,
            attn_other,
            vision_out_weight,
            out_weight_other,
        ),
        smem=1,
    )
    step3 = around([(i % 2, block) for i, block in enumerate(step2)])
    back1 = flipped(jnp.where(even, text, back2), "seq", 1)
    before_mine = shifted(norm_half, "seq", 1)
    before_other = other_core(before_mine)
    if rings:
        up, down = [block for block in (step3[0], step3[-1])]
        step4 = around([(0, up[:half]), (1, down[-half:])])
    if rings:
        at = lambda p: jnp.where(p % n < n // 2, 2 * (p % n), 2 * (n - 1 - p % n) + 1) * rows
        place = jnp.where(even, seq // 2, n - 1 - seq // 2)
        pieces = [(w, seq * rows)]
        for k, step in ((1, step1), (2, step2), (3, step3)):
            for i, block in enumerate(step):
                first = at(place + (k if i % 2 else n - k)) + i // 2 * (rows // chunks)
                pieces += [(block, first)]
        late, late_at = list(step4), at(place + n // 2)
    else:
        pieces = [(lax.all_gather(w, "seq", axis=0, tiled=True), 0)]
        late, late_at = [], 0

    gate = jnp.repeat(jnp.tanh(cross_gate), HEAD_SIZE)[None, :]
    place = jnp.stack([seq, core] + [jnp.asarray(p, jnp.int32) for p in (late_at, *[p[1] for p in pieces])])
    image = [sds((2 * tile_rows, 2 * kv_cols), F32)]
    if late:
        image.append(sds((2 * tile_rows, rows), BF16))
    image = list(call(
        functools.partial(image_kernel, len(pieces), rows if late else 0),
        tuple(image),
        (place, norm, before_mine, before_other, *[p[0] for p in pieces]),
        smem=1,
        scratch=(pltpu.VMEM((width, 2 * kv_cols), BF16),),
    ))
    turn, image[0] = lax.optimization_barrier((seq.reshape(1), image[0]))
    self_out = call(
        self_kernel,
        sds(text_query_rows.shape, F32),
        (turn, text_query_rows, text, back1, back2),
        smem=1,
    )
    return call(
        cross_kernel,
        sds(text_query_rows.shape, BF16),
        (seq.reshape(1), text_query_rows, self_out, tile_span.T, gate, *image, *late),
        smem=1,
        hbm=2,
        scratch=(
            pltpu.VMEM((2 * tile_rows, 2 * kv_cols), BF16),
            pltpu.VMEM(text_query_rows.shape, BF16),
            pltpu.VMEM(text_query_rows.shape, F32),
            pltpu.VMEM(text_query_rows.shape, BF16),
            pltpu.SemaphoreType.DMA((2 + kv_heads,)),
        ),
    )


def solution(mesh):
    placed = (
        P(("groups", "seq"), "head"),
        P(None, ("groups", "seq"), "head"),
        P(("groups", "seq")),
        P(("groups", "seq"), None),
        P(("groups", "seq"), None),
        P(None, ("groups", "seq"), "head"),
        P("head", None),
        P("seq", None, "head"),
        P("head"),
    )
    return jax.shard_map(
        per_device,
        mesh=mesh,
        in_specs=placed,
        out_specs=P(("groups", "seq"), "head"),
        check_vma=False,
    )
```

```python
import functools
import math

import jax
import jax.numpy as jnp
from jax import lax
from jax.experimental import pallas as pl
from jax.experimental.pallas import tpu as pltpu
from jax.sharding import PartitionSpec as P

HEAD_SIZE = 128
VHD = 80
LANES = 128
WINDOW_BLOCKS = 2
ID_ROWS = 16
NEG = -1e30
LOG2E = math.log2(math.e)
F32 = jnp.float32
BF16 = jnp.bfloat16
PLANNED_FLOPS = 20000000000
VMEM_LIMIT = 40 * 1024 * 1024


def dot_t(a, b):
    return lax.dot_general(a, b, (((1,), (1,)), ((), ())), preferred_element_type=F32)


def dot_n(a, b):
    return lax.dot_general(a, b, (((1,), (0,)), ((), ())), preferred_element_type=F32)


def column_of(row):
    n = row.shape[1]
    at = lax.broadcasted_iota(jnp.int32, (n, n), 0) == lax.broadcasted_iota(jnp.int32, (n, n), 1)
    return jnp.sum(jnp.where(at, row, 0.0), axis=1, keepdims=True)


def call(kernel, out_shape, args, smem=0, stored=False, scratch=()):
    many = isinstance(out_shape, (tuple, list))
    vmem = pl.BlockSpec(memory_space=pltpu.VMEM)
    anywhere = pl.BlockSpec(memory_space=pl.ANY)
    outs = out_shape if many else (out_shape,)
    moved = sum(math.prod(a.shape) * jnp.dtype(a.dtype).itemsize for a in (*args, *outs))
    return pl.pallas_call(
        kernel,
        out_shape=out_shape,
        in_specs=[pl.BlockSpec(memory_space=pltpu.SMEM)] * smem + [vmem] * (len(args) - smem),
        out_specs=[vmem] * len(out_shape) if many else anywhere if stored else vmem,
        scratch_shapes=list(scratch),
        compiler_params=pltpu.CompilerParams(vmem_limit_bytes=VMEM_LIMIT),
        cost_estimate=pl.CostEstimate(flops=PLANNED_FLOPS, bytes_accessed=moved, transcendentals=0),
    )(*args)


def vision_kernel(qkv, out):
    rows, cols = out.shape
    tiles = cols // LANES
    acc = [None] * tiles
    scale = LOG2E / math.sqrt(VHD)
    for head in range(cols // VHD):
        first, last = head * VHD, (head + 1) * VHD
        t0, t1 = first // LANES, -(-last // LANES)
        lanes = slice(t0 * LANES, t1 * LANES)
        lane = lax.broadcasted_iota(jnp.int32, (rows, (t1 - t0) * LANES), 1) + t0 * LANES
        mine = (lane >= first) & (lane < last)
        q = jnp.where(mine, qkv[0, :, lanes], jnp.zeros((), BF16))
        v = jnp.where(mine, qkv[2, :, lanes], jnp.zeros((), BF16))
        s = dot_t(q, qkv[1, :, lanes])
        p = jnp.exp2((s - jnp.max(s, axis=1, keepdims=True)) * scale)
        total = jnp.sum(p, axis=1, keepdims=True)
        o = dot_n(p.astype(BF16), v) * (1.0 / total)
        for t in range(t0, t1):
            part = o[:, (t - t0) * LANES : (t - t0 + 1) * LANES]
            acc[t] = part if acc[t] is None else acc[t] + part
    for t in range(tiles):
        out[:, t * LANES : (t + 1) * LANES] = acc[t].astype(BF16)


def rows_kernel(w, out):
    cols = w.shape[2]
    out[:, 0:cols] = w[:, 0, :]
    out[:, cols : 2 * cols] = w[:, 1, :]


def norm_kernel(core, hidden, attn_own, attn_other, w_own, w_other, out, half):
    mixed = (
        hidden[...].astype(F32)
        + dot_n(attn_own[...], w_own[...])
        + dot_n(attn_other[...], w_other[...])
    )
    mean = jnp.mean(mixed * mixed, axis=1, keepdims=True)
    out[...] = (mixed * lax.rsqrt(mean + 1e-05)).astype(BF16)
    n = half.shape[0]
    half[...] = out[pl.ds(pl.multiple_of(core[0] * n, n), n), :]


def stacked_queries(q, group, ratio):
    first = group * ratio * HEAD_SIZE
    return jnp.concatenate(
        [q[:, first + i * HEAD_SIZE : first + (i + 1) * HEAD_SIZE] for i in range(ratio)], axis=0
    )


def self_kernel(seq, q, own, back1, back2, out):
    rows = q.shape[0]
    groups = own.shape[1] // HEAD_SIZE
    ratio = q.shape[1] // HEAD_SIZE // groups
    scale = LOG2E / math.sqrt(HEAD_SIZE)
    blocks = (back2, back1, own)
    ids = [b[2 * rows : 2 * rows + ID_ROWS, 0:rows][0:1].astype(F32) for b in blocks]
    own_ids = column_of(ids[2])
    t = lax.broadcasted_iota(jnp.int32, (rows, rows), 0)
    k = lax.broadcasted_iota(jnp.int32, (rows, rows), 1)
    ok = [
        (ids[0] == own_ids) & (seq[0] >= 2),
        (ids[1] == own_ids) & (seq[0] >= 1),
        (ids[2] == own_ids) & (k <= t),
    ]
    bias = jnp.concatenate([jnp.where(m, 0.0, NEG) for m in ok], axis=1)
    bias = jnp.concatenate([bias] * ratio, axis=0)
    ones = jnp.ones((len(blocks) * rows, HEAD_SIZE), BF16)
    for g in range(groups):
        cols = slice(g * HEAD_SIZE, (g + 1) * HEAD_SIZE)
        keys = jnp.concatenate([b[0:rows, cols] for b in blocks], axis=0)
        values = jnp.concatenate([b[rows : 2 * rows, cols] for b in blocks], axis=0)
        s = dot_t(stacked_queries(q, g, ratio), keys) + bias
        p = jnp.exp2((s - jnp.max(s, axis=1, keepdims=True)) * scale).astype(BF16)
        o = dot_n(p, jnp.concatenate([values, ones], axis=1))
        o = o[:, :HEAD_SIZE] * (1.0 / o[:, HEAD_SIZE:])
        for i in range(ratio):
            j = g * ratio + i
            out[:, j * HEAD_SIZE : (j + 1) * HEAD_SIZE] = o[i * rows : (i + 1) * rows]


def image_kernel(pieces, late, place, norm_own, before_mine, before_other, *refs):
    weights, refs = refs[:pieces], refs[pieces:]
    total, w = refs[0], refs[-1]
    for i, piece in enumerate(weights):
        n = piece.shape[0]
        w[pl.ds(pl.multiple_of(place[3 + i], ID_ROWS), n), :] = piece[...]
    first, mine, other = place[1] == 0, before_mine[...], before_other[...]
    norms = [jnp.where(first, mine, other), jnp.where(first, other, mine), norm_own[...]]
    norms = jnp.concatenate(norms, axis=0)
    if late:
        w[pl.ds(pl.multiple_of(place[2], ID_ROWS), late), :] = jnp.zeros((late, w.shape[1]), BF16)
        shape = (w.shape[0], late)
        picks = lax.broadcasted_iota(jnp.int32, shape, 0) == (
            lax.broadcasted_iota(jnp.int32, shape, 1) + place[2]
        )
        refs[1][...] = dot_n(norms, jnp.where(picks, 1.0, 0.0).astype(BF16)).astype(BF16)
    total[...] = dot_n(norms, w[...])


def cross_kernel(seq, q, self_out, span, gate, total, *refs):
    late, (out_all, kv, out, sems) = refs[:-4], refs[-4:]
    rows = q.shape[0]
    tile = total.shape[0] // 2
    kv_cols = total.shape[1] // 2
    groups = kv_cols // HEAD_SIZE
    ratio = q.shape[1] // HEAD_SIZE // groups
    scale = LOG2E / math.sqrt(HEAD_SIZE)
    if late:
        rest = jnp.concatenate([block[...] for block in late[1:]], axis=0)
        kv[...] = (total[...] + dot_n(late[0][...], rest)).astype(BF16)
    else:
        kv[...] = total[...].astype(BF16)
    this = seq[0].astype(F32)
    low = column_of(span[0:1, :].astype(F32))
    high = column_of(span[1:2, :].astype(F32))
    see_own = (low <= this) & (this < high)
    see_before = (low <= this - 1.0) & (this - 1.0 < high)
    present = jnp.broadcast_to(jnp.where(low < high, 1.0, 0.0), (rows, HEAD_SIZE))
    bias = jnp.concatenate(
        [
            jnp.broadcast_to(jnp.where(see, 0.0, NEG), (rows, tile))
            for see in (see_before, see_own)
        ],
        axis=1,
    )
    ones = jnp.ones((2 * tile, HEAD_SIZE), BF16)
    stores = []
    for g in range(groups):
        keys = kv[:, g * HEAD_SIZE : (g + 1) * HEAD_SIZE]
        values = kv[:, kv_cols + g * HEAD_SIZE : kv_cols + (g + 1) * HEAD_SIZE]
        values = jnp.concatenate([values, ones], axis=1)
        for i in range(ratio):
            at = slice((g * ratio + i) * HEAD_SIZE, (g * ratio + i + 1) * HEAD_SIZE)
            s = dot_t(q[:, at], keys) + bias
            p = jnp.exp2((s - jnp.max(s, axis=1, keepdims=True)) * scale).astype(BF16)
            o = dot_n(p, values)
            o = o[:, :HEAD_SIZE] * (1.0 / o[:, HEAD_SIZE:])
            out[:, at] = (self_out[:, at] + gate[:, at] * present * o).astype(BF16)
        whole = slice(g * ratio * HEAD_SIZE, (g + 1) * ratio * HEAD_SIZE)
        stores.append(pltpu.make_async_copy(out.at[:, whole], out_all.at[:, whole], sems.at[g]))
        stores[-1].start()
    for store in stores:
        store.wait()


def shifted(block, axis, distance):
    n = lax.axis_size(axis)
    return lax.ppermute(block, axis, [(i, i + distance) for i in range(n - distance)])


def flipped(block, axis, bits):
    return lax.ppermute(block, axis, [(i, i ^ bits) for i in range(lax.axis_size(axis))])


def per_device(
    text_query_rows,
    text_key_value,
    doc_ids,
    tile_span,
    vision_hidden,
    vision_qkv,
    vision_out_weight,
    cross_keyvalue_weight,
    cross_gate,
):
    text_rows = text_query_rows.shape[0]
    tile_rows, width = vision_hidden.shape
    kv_cols = text_key_value.shape[2]
    kv_heads = kv_cols // HEAD_SIZE
    q_heads = text_query_rows.shape[1] // HEAD_SIZE
    seq = lax.axis_index("seq")
    core = lax.axis_index("head")
    other_core = functools.partial(flipped, axis="head", bits=1)
    sds = jax.ShapeDtypeStruct

    rows = cross_keyvalue_weight.shape[0]
    n = lax.axis_size("seq")
    half = rows // 2
    ring = [i for i in range(0, n, 2)] + [i for i in range(n - 1, 0, -2)]
    rings = n == 8 and rows % 32 == 0
    even = seq % 2 == 0

    chunks = 1
    ways = [(ring[i - 1], ring[i]) for i in range(n)], [(ring[i], ring[i - 1]) for i in range(n)]

    def around(blocks):
        return [lax.ppermute(block, "seq", ways[way]) for way, block in blocks] if rings else []

    ids = jnp.broadcast_to(doc_ids.astype(BF16), (ID_ROWS, text_rows))
    ids = jnp.pad(ids, ((0, 0), (0, kv_cols - text_rows)))
    text = jnp.concatenate([text_key_value.reshape(-1, kv_cols), ids], axis=0)
    (w,) = call(
        rows_kernel,
        (sds((rows, 2 * kv_cols), BF16),),
        (cross_keyvalue_weight,),
    )
    out_weight_other = other_core(vision_out_weight)
    step1 = around([(way, w[c * rows // chunks : (c + 1) * rows // chunks]) for c in range(chunks) for way in (0, 1)])
    attn = call(
        vision_kernel,
        sds((tile_rows, vision_qkv.shape[2]), BF16),
        (vision_qkv,),
    )
    attn_other = other_core(attn)
    back2 = shifted(text, "seq", 2)
    step2 = around([(i % 2, block) for i, block in enumerate(step1)])
    norm, norm_half = call(
        norm_kernel,
        (sds((tile_rows, width), BF16), sds((tile_rows // 2, width), BF16)),
        (
            core.reshape(1),
            vision_hidden,
            attn,
            attn_other,
            vision_out_weight,
            out_weight_other,
        ),
        smem=1,
    )
    step3 = around([(i % 2, block) for i, block in enumerate(step2)])
    back1 = flipped(jnp.where(even, text, back2), "seq", 1)
    before_mine = shifted(norm_half, "seq", 1)
    before_other = other_core(before_mine)
    if rings:
        up, down = [block for block in (step3[0], step3[-1])]
        step4 = around([(0, up[:half]), (1, down[-half:])])
    if rings:
        at = lambda p: jnp.where(p % n < n // 2, 2 * (p % n), 2 * (n - 1 - p % n) + 1) * rows
        place = jnp.where(even, seq // 2, n - 1 - seq // 2)
        pieces = [(w, seq * rows)]
        for k, step in ((1, step1), (2, step2), (3, step3)):
            for i, block in enumerate(step):
                first = at(place + (k if i % 2 else n - k)) + i // 2 * (rows // chunks)
                pieces += [(block, first)]
        late, late_at = list(step4), at(place + n // 2)
    else:
        pieces = [(lax.all_gather(w, "seq", axis=0, tiled=True), 0)]
        late, late_at = [], 0

    gate = jnp.repeat(jnp.tanh(cross_gate), HEAD_SIZE)[None, :]
    place = jnp.stack([seq, core] + [jnp.asarray(p, jnp.int32) for p in (late_at, *[p[1] for p in pieces])])
    image = [sds((2 * tile_rows, 2 * kv_cols), F32)]
    if late:
        image.append(sds((2 * tile_rows, rows), BF16))
    image = list(call(
        functools.partial(image_kernel, len(pieces), rows if late else 0),
        tuple(image),
        (place, norm, before_mine, before_other, *[p[0] for p in pieces]),
        smem=1,
        scratch=(pltpu.VMEM((width, 2 * kv_cols), BF16),),
    ))
    turn, image[0] = lax.optimization_barrier((seq.reshape(1), image[0]))
    self_out = call(
        self_kernel,
        sds(text_query_rows.shape, F32),
        (turn, text_query_rows, text, back1, back2),
        smem=1,
    )
    return call(
        cross_kernel,
        sds(text_query_rows.shape, BF16),
        (seq.reshape(1), text_query_rows, self_out, tile_span.T, gate, *image, *late),
        smem=1,
        stored=True,
        scratch=(
            pltpu.VMEM((2 * tile_rows, 2 * kv_cols), BF16),
            pltpu.VMEM(text_query_rows.shape, BF16),
            pltpu.SemaphoreType.DMA((kv_heads,)),
        ),
    )


def solution(mesh):
    placed = (
        P(("groups", "seq"), "head"),
        P(None, ("groups", "seq"), "head"),
        P(("groups", "seq")),
        P(("groups", "seq"), None),
        P(("groups", "seq"), None),
        P(None, ("groups", "seq"), "head"),
        P("head", None),
        P("seq", None, "head"),
        P("head"),
    )
    return jax.shard_map(
        per_device,
        mesh=mesh,
        in_specs=placed,
        out_specs=P(("groups", "seq"), "head"),
        check_vma=False,
    )
```

```python
import functools
import math

import jax
import jax.numpy as jnp
from jax import lax
from jax.experimental import pallas as pl
from jax.experimental.pallas import tpu as pltpu
from jax.sharding import PartitionSpec as P

HEAD_SIZE = 128
VHD = 80
LANES = 128
WINDOW_BLOCKS = 2
ID_ROWS = 16
NEG = -1e30
LOG2E = math.log2(math.e)
F32 = jnp.float32
BF16 = jnp.bfloat16
PLANNED_FLOPS = 20000000000
VMEM_LIMIT = 40 * 1024 * 1024


def dot_t(a, b):
    return lax.dot_general(a, b, (((1,), (1,)), ((), ())), preferred_element_type=F32)


def dot_n(a, b):
    return lax.dot_general(a, b, (((1,), (0,)), ((), ())), preferred_element_type=F32)


def column_of(row):
    n = row.shape[1]
    at = lax.broadcasted_iota(jnp.int32, (n, n), 0) == lax.broadcasted_iota(jnp.int32, (n, n), 1)
    return jnp.sum(jnp.where(at, row, 0.0), axis=1, keepdims=True)


def call(kernel, out_shape, args, smem=0, stored=False, scratch=()):
    many = isinstance(out_shape, (tuple, list))
    vmem = pl.BlockSpec(memory_space=pltpu.VMEM)
    anywhere = pl.BlockSpec(memory_space=pl.ANY)
    outs = out_shape if many else (out_shape,)
    moved = sum(math.prod(a.shape) * jnp.dtype(a.dtype).itemsize for a in (*args, *outs))
    return pl.pallas_call(
        kernel,
        out_shape=out_shape,
        in_specs=[pl.BlockSpec(memory_space=pltpu.SMEM)] * smem + [vmem] * (len(args) - smem),
        out_specs=[vmem] * len(out_shape) if many else anywhere if stored else vmem,
        scratch_shapes=list(scratch),
        compiler_params=pltpu.CompilerParams(vmem_limit_bytes=VMEM_LIMIT),
        cost_estimate=pl.CostEstimate(flops=PLANNED_FLOPS, bytes_accessed=moved, transcendentals=0),
    )(*args)


def vision_kernel(qkv, out):
    rows, cols = out.shape
    tiles = cols // LANES
    acc = [None] * tiles
    scale = LOG2E / math.sqrt(VHD)
    for head in range(cols // VHD):
        first, last = head * VHD, (head + 1) * VHD
        t0, t1 = first // LANES, -(-last // LANES)
        lanes = slice(t0 * LANES, t1 * LANES)
        lane = lax.broadcasted_iota(jnp.int32, (rows, (t1 - t0) * LANES), 1) + t0 * LANES
        mine = (lane >= first) & (lane < last)
        q = jnp.where(mine, qkv[0, :, lanes], jnp.zeros((), BF16))
        v = jnp.where(mine, qkv[2, :, lanes], jnp.zeros((), BF16))
        s = dot_t(q, qkv[1, :, lanes])
        p = jnp.exp2((s - jnp.max(s, axis=1, keepdims=True)) * scale)
        total = jnp.sum(p, axis=1, keepdims=True)
        o = dot_n(p.astype(BF16), v) * (1.0 / total)
        for t in range(t0, t1):
            part = o[:, (t - t0) * LANES : (t - t0 + 1) * LANES]
            acc[t] = part if acc[t] is None else acc[t] + part
    for t in range(tiles):
        out[:, t * LANES : (t + 1) * LANES] = acc[t].astype(BF16)


def rows_kernel(w, out):
    cols = w.shape[2]
    out[:, 0:cols] = w[:, 0, :]
    out[:, cols : 2 * cols] = w[:, 1, :]


def norm_kernel(core, hidden, attn_own, attn_other, w_own, w_other, out, half):
    mixed = (
        hidden[...].astype(F32)
        + dot_n(attn_own[...], w_own[...])
        + dot_n(attn_other[...], w_other[...])
    )
    mean = jnp.mean(mixed * mixed, axis=1, keepdims=True)
    out[...] = (mixed * lax.rsqrt(mean + 1e-05)).astype(BF16)
    n = half.shape[0]
    half[...] = out[pl.ds(pl.multiple_of(core[0] * n, n), n), :]


def self_kernel(seq, q, own, back1, back2, out):
    rows = q.shape[0]
    groups = own.shape[1] // HEAD_SIZE
    ratio = q.shape[1] // HEAD_SIZE // groups
    scale = LOG2E / math.sqrt(HEAD_SIZE)
    blocks = (back2, back1, own)
    ids = [b[2 * rows : 2 * rows + ID_ROWS, 0:rows][0:1].astype(F32) for b in blocks]
    own_ids = column_of(ids[2])
    t = lax.broadcasted_iota(jnp.int32, (rows, rows), 0)
    k = lax.broadcasted_iota(jnp.int32, (rows, rows), 1)
    ok = [
        (ids[0] == own_ids) & (seq[0] >= 2),
        (ids[1] == own_ids) & (seq[0] >= 1),
        (ids[2] == own_ids) & (k <= t),
    ]
    bias = jnp.concatenate([jnp.where(m, 0.0, NEG) for m in ok], axis=1)
    ones = jnp.ones((len(blocks) * rows, HEAD_SIZE), BF16)
    for g in range(groups):
        cols = slice(g * HEAD_SIZE, (g + 1) * HEAD_SIZE)
        keys = jnp.concatenate([b[0:rows, cols] for b in blocks], axis=0)
        values = jnp.concatenate([b[rows : 2 * rows, cols] for b in blocks], axis=0)
        values = jnp.concatenate([values, ones], axis=1)
        for i in range(ratio):
            at = slice((g * ratio + i) * HEAD_SIZE, (g * ratio + i + 1) * HEAD_SIZE)
            s = dot_t(q[:, at], keys) + bias
            p = jnp.exp2((s - jnp.max(s, axis=1, keepdims=True)) * scale).astype(BF16)
            o = dot_n(p, values)
            out[:, at] = o[:, :HEAD_SIZE] * (1.0 / o[:, HEAD_SIZE:])


def image_kernel(pieces, late, place, norm_own, before_mine, before_other, *refs):
    weights, refs = refs[:pieces], refs[pieces:]
    total, w = refs[0], refs[-1]
    for i, piece in enumerate(weights):
        n = piece.shape[0]
        w[pl.ds(pl.multiple_of(place[3 + i], ID_ROWS), n), :] = piece[...]
    first, mine, other = place[1] == 0, before_mine[...], before_other[...]
    norms = [jnp.where(first, mine, other), jnp.where(first, other, mine), norm_own[...]]
    norms = jnp.concatenate(norms, axis=0)
    if late:
        w[pl.ds(pl.multiple_of(place[2], ID_ROWS), late), :] = jnp.zeros((late, w.shape[1]), BF16)
        shape = (w.shape[0], late)
        picks = lax.broadcasted_iota(jnp.int32, shape, 0) == (
            lax.broadcasted_iota(jnp.int32, shape, 1) + place[2]
        )
        refs[1][...] = dot_n(norms, jnp.where(picks, 1.0, 0.0).astype(BF16)).astype(BF16)
    total[...] = dot_n(norms, w[...])


def cross_kernel(seq, q, self_out, span, gate, total, *refs):
    late, (out_all, kv, out, sems) = refs[:-4], refs[-4:]
    rows = q.shape[0]
    tile = total.shape[0] // 2
    kv_cols = total.shape[1] // 2
    groups = kv_cols // HEAD_SIZE
    ratio = q.shape[1] // HEAD_SIZE // groups
    scale = LOG2E / math.sqrt(HEAD_SIZE)
    if late:
        rest = jnp.concatenate([block[...] for block in late[1:]], axis=0)
        kv[...] = (total[...] + dot_n(late[0][...], rest)).astype(BF16)
    else:
        kv[...] = total[...].astype(BF16)
    this = seq[0].astype(F32)
    low = column_of(span[0:1, :].astype(F32))
    high = column_of(span[1:2, :].astype(F32))
    see_own = (low <= this) & (this < high)
    see_before = (low <= this - 1.0) & (this - 1.0 < high)
    present = jnp.broadcast_to(jnp.where(low < high, 1.0, 0.0), (rows, HEAD_SIZE))
    bias = jnp.concatenate(
        [
            jnp.broadcast_to(jnp.where(see, 0.0, NEG), (rows, tile))
            for see in (see_before, see_own)
        ],
        axis=1,
    )
    ones = jnp.ones((2 * tile, HEAD_SIZE), BF16)
    stores = []
    for g in range(groups):
        keys = kv[:, g * HEAD_SIZE : (g + 1) * HEAD_SIZE]
        values = kv[:, kv_cols + g * HEAD_SIZE : kv_cols + (g + 1) * HEAD_SIZE]
        values = jnp.concatenate([values, ones], axis=1)
        for i in range(ratio):
            at = slice((g * ratio + i) * HEAD_SIZE, (g * ratio + i + 1) * HEAD_SIZE)
            s = dot_t(q[:, at], keys) + bias
            p = jnp.exp2((s - jnp.max(s, axis=1, keepdims=True)) * scale).astype(BF16)
            o = dot_n(p, values)
            o = o[:, :HEAD_SIZE] * (1.0 / o[:, HEAD_SIZE:])
            out[:, at] = (self_out[:, at] + gate[:, at] * present * o).astype(BF16)
        whole = slice(g * ratio * HEAD_SIZE, (g + 1) * ratio * HEAD_SIZE)
        stores.append(pltpu.make_async_copy(out.at[:, whole], out_all.at[:, whole], sems.at[g]))
        stores[-1].start()
    for store in stores:
        store.wait()


def shifted(block, axis, distance):
    n = lax.axis_size(axis)
    return lax.ppermute(block, axis, [(i, i + distance) for i in range(n - distance)])


def flipped(block, axis, bits):
    return lax.ppermute(block, axis, [(i, i ^ bits) for i in range(lax.axis_size(axis))])


def per_device(
    text_query_rows,
    text_key_value,
    doc_ids,
    tile_span,
    vision_hidden,
    vision_qkv,
    vision_out_weight,
    cross_keyvalue_weight,
    cross_gate,
):
    text_rows = text_query_rows.shape[0]
    tile_rows, width = vision_hidden.shape
    kv_cols = text_key_value.shape[2]
    kv_heads = kv_cols // HEAD_SIZE
    q_heads = text_query_rows.shape[1] // HEAD_SIZE
    seq = lax.axis_index("seq")
    core = lax.axis_index("head")
    other_core = functools.partial(flipped, axis="head", bits=1)
    sds = jax.ShapeDtypeStruct

    rows = cross_keyvalue_weight.shape[0]
    n = lax.axis_size("seq")
    half = rows // 2
    ring = [i for i in range(0, n, 2)] + [i for i in range(n - 1, 0, -2)]
    rings = n == 8 and rows % 32 == 0
    even = seq % 2 == 0

    chunks = 1
    ways = [(ring[i - 1], ring[i]) for i in range(n)], [(ring[i], ring[i - 1]) for i in range(n)]

    def around(blocks):
        return [lax.ppermute(block, "seq", ways[way]) for way, block in blocks] if rings else []

    ids = jnp.broadcast_to(doc_ids.astype(BF16), (ID_ROWS, text_rows))
    ids = jnp.pad(ids, ((0, 0), (0, kv_cols - text_rows)))
    text = jnp.concatenate([text_key_value.reshape(-1, kv_cols), ids], axis=0)
    (w,) = call(
        rows_kernel,
        (sds((rows, 2 * kv_cols), BF16),),
        (cross_keyvalue_weight,),
    )
    out_weight_other = other_core(vision_out_weight)
    step1 = around([(way, w[c * rows // chunks : (c + 1) * rows // chunks]) for c in range(chunks) for way in (0, 1)])
    attn = call(
        vision_kernel,
        sds((tile_rows, vision_qkv.shape[2]), BF16),
        (vision_qkv,),
    )
    attn_other = other_core(attn)
    back2 = shifted(text, "seq", 2)
    step2 = around([(i % 2, block) for i, block in enumerate(step1)])
    norm, norm_half = call(
        norm_kernel,
        (sds((tile_rows, width), BF16), sds((tile_rows // 2, width), BF16)),
        (
            core.reshape(1),
            vision_hidden,
            attn,
            attn_other,
            vision_out_weight,
            out_weight_other,
        ),
        smem=1,
    )
    step3 = around([(i % 2, block) for i, block in enumerate(step2)])
    back1 = flipped(jnp.where(even, text, back2), "seq", 1)
    before_mine = shifted(norm_half, "seq", 1)
    before_other = other_core(before_mine)
    if rings:
        up, down = [block for block in (step3[0], step3[-1])]
        step4 = around([(0, up[:half]), (1, down[-half:])])
    if rings:
        at = lambda p: jnp.where(p % n < n // 2, 2 * (p % n), 2 * (n - 1 - p % n) + 1) * rows
        place = jnp.where(even, seq // 2, n - 1 - seq // 2)
        pieces = [(w, seq * rows)]
        for k, step in ((1, step1), (2, step2), (3, step3)):
            for i, block in enumerate(step):
                first = at(place + (k if i % 2 else n - k)) + i // 2 * (rows // chunks)
                pieces += [(block, first)]
        late, late_at = list(step4), at(place + n // 2)
    else:
        pieces = [(lax.all_gather(w, "seq", axis=0, tiled=True), 0)]
        late, late_at = [], 0

    gate = jnp.repeat(jnp.tanh(cross_gate), HEAD_SIZE)[None, :]
    place = jnp.stack([seq, core] + [jnp.asarray(p, jnp.int32) for p in (late_at, *[p[1] for p in pieces])])
    image = [sds((2 * tile_rows, 2 * kv_cols), F32)]
    if late:
        image.append(sds((2 * tile_rows, rows), BF16))
    image = list(call(
        functools.partial(image_kernel, len(pieces), rows if late else 0),
        tuple(image),
        (place, norm, before_mine, before_other, *[p[0] for p in pieces]),
        smem=1,
        scratch=(pltpu.VMEM((width, 2 * kv_cols), BF16),),
    ))
    turn, image[0] = lax.optimization_barrier((seq.reshape(1), image[0]))
    self_out = call(
        self_kernel,
        sds(text_query_rows.shape, F32),
        (turn, text_query_rows, text, back1, back2),
        smem=1,
    )
    return call(
        cross_kernel,
        sds(text_query_rows.shape, BF16),
        (seq.reshape(1), text_query_rows, self_out, tile_span.T, gate, *image, *late),
        smem=1,
        stored=True,
        scratch=(
            pltpu.VMEM((2 * tile_rows, 2 * kv_cols), BF16),
            pltpu.VMEM(text_query_rows.shape, BF16),
            pltpu.SemaphoreType.DMA((kv_heads,)),
        ),
    )


def solution(mesh):
    placed = (
        P(("groups", "seq"), "head"),
        P(None, ("groups", "seq"), "head"),
        P(("groups", "seq")),
        P(("groups", "seq"), None),
        P(("groups", "seq"), None),
        P(None, ("groups", "seq"), "head"),
        P("head", None),
        P("seq", None, "head"),
        P("head"),
    )
    return jax.shard_map(
        per_device,
        mesh=mesh,
        in_specs=placed,
        out_specs=P(("groups", "seq"), "head"),
        check_vma=False,
    )
```

```python
import functools
import math

import jax
import jax.numpy as jnp
from jax import lax
from jax.experimental import pallas as pl
from jax.experimental.pallas import tpu as pltpu
from jax.sharding import PartitionSpec as P

HEAD_SIZE = 128
VHD = 80
LANES = 128
WINDOW_BLOCKS = 2
ID_ROWS = 16
NEG = -1e30
LOG2E = math.log2(math.e)
F32 = jnp.float32
BF16 = jnp.bfloat16
PLANNED_FLOPS = 20000000000
VMEM_LIMIT = 32 * 1024 * 1024


def dot_t(a, b):
    return lax.dot_general(a, b, (((1,), (1,)), ((), ())), preferred_element_type=F32)


def dot_n(a, b):
    return lax.dot_general(a, b, (((1,), (0,)), ((), ())), preferred_element_type=F32)


def column_of(row):
    n = row.shape[1]
    at = lax.broadcasted_iota(jnp.int32, (n, n), 0) == lax.broadcasted_iota(jnp.int32, (n, n), 1)
    return jnp.sum(jnp.where(at, row, 0.0), axis=1, keepdims=True)


def call(kernel, out_shape, args, smem=0, stored=False, scratch=()):
    many = isinstance(out_shape, (tuple, list))
    vmem = pl.BlockSpec(memory_space=pltpu.VMEM)
    anywhere = pl.BlockSpec(memory_space=pl.ANY)
    outs = out_shape if many else (out_shape,)
    moved = sum(math.prod(a.shape) * jnp.dtype(a.dtype).itemsize for a in (*args, *outs))
    return pl.pallas_call(
        kernel,
        out_shape=out_shape,
        in_specs=[pl.BlockSpec(memory_space=pltpu.SMEM)] * smem + [vmem] * (len(args) - smem),
        out_specs=[vmem] * len(out_shape) if many else anywhere if stored else vmem,
        scratch_shapes=list(scratch),
        compiler_params=pltpu.CompilerParams(vmem_limit_bytes=VMEM_LIMIT),
        cost_estimate=pl.CostEstimate(flops=PLANNED_FLOPS, bytes_accessed=moved, transcendentals=0),
    )(*args)


def vision_kernel(qkv, out):
    rows, cols = out.shape
    tiles = cols // LANES
    acc = [None] * tiles
    scale = LOG2E / math.sqrt(VHD)
    for head in range(cols // VHD):
        first, last = head * VHD, (head + 1) * VHD
        t0, t1 = first // LANES, -(-last // LANES)
        lanes = slice(t0 * LANES, t1 * LANES)
        lane = lax.broadcasted_iota(jnp.int32, (rows, (t1 - t0) * LANES), 1) + t0 * LANES
        mine = (lane >= first) & (lane < last)
        q = jnp.where(mine, qkv[0, :, lanes], jnp.zeros((), BF16))
        v = jnp.where(mine, qkv[2, :, lanes], jnp.zeros((), BF16))
        s = dot_t(q, qkv[1, :, lanes])
        p = jnp.exp2((s - jnp.max(s, axis=1, keepdims=True)) * scale)
        total = jnp.sum(p, axis=1, keepdims=True)
        o = dot_n(p.astype(BF16), v) * (1.0 / total)
        for t in range(t0, t1):
            part = o[:, (t - t0) * LANES : (t - t0 + 1) * LANES]
            acc[t] = part if acc[t] is None else acc[t] + part
    for t in range(tiles):
        out[:, t * LANES : (t + 1) * LANES] = acc[t].astype(BF16)


def rows_kernel(w, out):
    cols = w.shape[2]
    out[:, 0:cols] = w[:, 0, :]
    out[:, cols : 2 * cols] = w[:, 1, :]


def norm_kernel(core, hidden, attn_own, attn_other, w_own, w_other, out, half):
    mixed = (
        hidden[...].astype(F32)
        + dot_n(attn_own[...], w_own[...])
        + dot_n(attn_other[...], w_other[...])
    )
    mean = jnp.mean(mixed * mixed, axis=1, keepdims=True)
    out[...] = (mixed * lax.rsqrt(mean + 1e-05)).astype(BF16)
    n = half.shape[0]
    half[...] = out[pl.ds(pl.multiple_of(core[0] * n, n), n), :]


def self_kernel(seq, q, own, back1, back2, out):
    rows = q.shape[0]
    groups = own.shape[1] // HEAD_SIZE
    ratio = q.shape[1] // HEAD_SIZE // groups
    scale = LOG2E / math.sqrt(HEAD_SIZE)
    blocks = (back2, back1, own)
    ids = [b[2 * rows : 2 * rows + ID_ROWS, 0:rows][0:1].astype(F32) for b in blocks]
    own_ids = column_of(ids[2])
    t = lax.broadcasted_iota(jnp.int32, (rows, rows), 0)
    k = lax.broadcasted_iota(jnp.int32, (rows, rows), 1)
    ok = [
        (ids[0] == own_ids) & (seq[0] >= 2),
        (ids[1] == own_ids) & (seq[0] >= 1),
        (ids[2] == own_ids) & (k <= t),
    ]
    bias = jnp.concatenate([jnp.where(m, 0.0, NEG) for m in ok], axis=1)
    ones = jnp.ones((len(blocks) * rows, HEAD_SIZE), BF16)
    for g in range(groups):
        cols = slice(g * HEAD_SIZE, (g + 1) * HEAD_SIZE)
        keys = jnp.concatenate([b[0:rows, cols] for b in blocks], axis=0)
        values = jnp.concatenate([b[rows : 2 * rows, cols] for b in blocks], axis=0)
        values = jnp.concatenate([values, ones], axis=1)
        for i in range(ratio):
            at = slice((g * ratio + i) * HEAD_SIZE, (g * ratio + i + 1) * HEAD_SIZE)
            s = dot_t(q[:, at], keys) + bias
            p = jnp.exp2((s - jnp.max(s, axis=1, keepdims=True)) * scale).astype(BF16)
            o = dot_n(p, values)
            out[:, at] = o[:, :HEAD_SIZE] * (1.0 / o[:, HEAD_SIZE:])


def image_kernel(pieces, late, place, norm_own, before_mine, before_other, *refs):
    weights, refs = refs[:pieces], refs[pieces:]
    total, w = refs[0], refs[-1]
    for i, piece in enumerate(weights):
        n = piece.shape[0]
        w[pl.ds(pl.multiple_of(place[3 + i], ID_ROWS), n), :] = piece[...]
    first, mine, other = place[1] == 0, before_mine[...], before_other[...]
    norms = [jnp.where(first, mine, other), jnp.where(first, other, mine), norm_own[...]]
    norms = jnp.concatenate(norms, axis=0)
    if late:
        w[pl.ds(pl.multiple_of(place[2], ID_ROWS), late), :] = jnp.zeros((late, w.shape[1]), BF16)
        shape = (w.shape[0], late)
        picks = lax.broadcasted_iota(jnp.int32, shape, 0) == (
            lax.broadcasted_iota(jnp.int32, shape, 1) + place[2]
        )
        refs[1][...] = dot_n(norms, jnp.where(picks, 1.0, 0.0).astype(BF16)).astype(BF16)
    total[...] = dot_n(norms, w[...])


def cross_kernel(seq, q, self_out, span, gate, total, *refs):
    late, (out_all, kv, out, sems) = refs[:-4], refs[-4:]
    rows = q.shape[0]
    tile = total.shape[0] // 2
    kv_cols = total.shape[1] // 2
    groups = kv_cols // HEAD_SIZE
    ratio = q.shape[1] // HEAD_SIZE // groups
    scale = LOG2E / math.sqrt(HEAD_SIZE)
    if late:
        rest = jnp.concatenate([block[...] for block in late[1:]], axis=0)
        kv[...] = (total[...] + dot_n(late[0][...], rest)).astype(BF16)
    else:
        kv[...] = total[...].astype(BF16)
    this = seq[0].astype(F32)
    low = column_of(span[0:1, :].astype(F32))
    high = column_of(span[1:2, :].astype(F32))
    see_own = (low <= this) & (this < high)
    see_before = (low <= this - 1.0) & (this - 1.0 < high)
    present = jnp.broadcast_to(jnp.where(low < high, 1.0, 0.0), (rows, HEAD_SIZE))
    bias = jnp.concatenate(
        [
            jnp.broadcast_to(jnp.where(see, 0.0, NEG), (rows, tile))
            for see in (see_before, see_own)
        ],
        axis=1,
    )
    ones = jnp.ones((2 * tile, HEAD_SIZE), BF16)
    stores = []
    for g in range(groups):
        keys = kv[:, g * HEAD_SIZE : (g + 1) * HEAD_SIZE]
        values = kv[:, kv_cols + g * HEAD_SIZE : kv_cols + (g + 1) * HEAD_SIZE]
        values = jnp.concatenate([values, ones], axis=1)
        for i in range(ratio):
            at = slice((g * ratio + i) * HEAD_SIZE, (g * ratio + i + 1) * HEAD_SIZE)
            s = dot_t(q[:, at], keys) + bias
            p = jnp.exp2((s - jnp.max(s, axis=1, keepdims=True)) * scale).astype(BF16)
            o = dot_n(p, values)
            o = o[:, :HEAD_SIZE] * (1.0 / o[:, HEAD_SIZE:])
            out[:, at] = (self_out[:, at] + gate[:, at] * present * o).astype(BF16)
        whole = slice(g * ratio * HEAD_SIZE, (g + 1) * ratio * HEAD_SIZE)
        stores.append(pltpu.make_async_copy(out.at[:, whole], out_all.at[:, whole], sems.at[g]))
        stores[-1].start()
    for store in stores:
        store.wait()


def shifted(block, axis, distance):
    n = lax.axis_size(axis)
    return lax.ppermute(block, axis, [(i, i + distance) for i in range(n - distance)])


def flipped(block, axis, bits):
    return lax.ppermute(block, axis, [(i, i ^ bits) for i in range(lax.axis_size(axis))])


def per_device(
    text_query_rows,
    text_key_value,
    doc_ids,
    tile_span,
    vision_hidden,
    vision_qkv,
    vision_out_weight,
    cross_keyvalue_weight,
    cross_gate,
):
    text_rows = text_query_rows.shape[0]
    tile_rows, width = vision_hidden.shape
    kv_cols = text_key_value.shape[2]
    kv_heads = kv_cols // HEAD_SIZE
    q_heads = text_query_rows.shape[1] // HEAD_SIZE
    seq = lax.axis_index("seq")
    core = lax.axis_index("head")
    other_core = functools.partial(flipped, axis="head", bits=1)
    sds = jax.ShapeDtypeStruct

    rows = cross_keyvalue_weight.shape[0]
    n = lax.axis_size("seq")
    half = rows // 2
    ring = [i for i in range(0, n, 2)] + [i for i in range(n - 1, 0, -2)]
    rings = n == 8 and rows % 32 == 0
    even = seq % 2 == 0

    chunks = 1
    ways = [(ring[i - 1], ring[i]) for i in range(n)], [(ring[i], ring[i - 1]) for i in range(n)]

    def around(blocks):
        return [lax.ppermute(block, "seq", ways[way]) for way, block in blocks] if rings else []

    ids = jnp.broadcast_to(doc_ids.astype(BF16), (ID_ROWS, text_rows))
    ids = jnp.pad(ids, ((0, 0), (0, kv_cols - text_rows)))
    text = jnp.concatenate([text_key_value.reshape(-1, kv_cols), ids], axis=0)
    (w,) = call(
        rows_kernel,
        (sds((rows, 2 * kv_cols), BF16),),
        (cross_keyvalue_weight,),
    )
    out_weight_other = other_core(vision_out_weight)
    step1 = around([(way, w[c * rows // chunks : (c + 1) * rows // chunks]) for c in range(chunks) for way in (0, 1)])
    attn = call(
        vision_kernel,
        sds((tile_rows, vision_qkv.shape[2]), BF16),
        (vision_qkv,),
    )
    attn_other = other_core(attn)
    back2 = shifted(text, "seq", 2)
    step2 = around([(i % 2, block) for i, block in enumerate(step1)])
    norm, norm_half = call(
        norm_kernel,
        (sds((tile_rows, width), BF16), sds((tile_rows // 2, width), BF16)),
        (
            core.reshape(1),
            vision_hidden,
            attn,
            attn_other,
            vision_out_weight,
            out_weight_other,
        ),
        smem=1,
    )
    step3 = around([(i % 2, block) for i, block in enumerate(step2)])
    back1 = flipped(jnp.where(even, text, back2), "seq", 1)
    before_mine = shifted(norm_half, "seq", 1)
    before_other = other_core(before_mine)
    if rings:
        up, down = [block for block in (step3[0], step3[-1])]
        step4 = around([(0, up[:half]), (1, down[-half:])])
    if rings:
        at = lambda p: jnp.where(p % n < n // 2, 2 * (p % n), 2 * (n - 1 - p % n) + 1) * rows
        place = jnp.where(even, seq // 2, n - 1 - seq // 2)
        pieces = [(w, seq * rows)]
        for k, step in ((1, step1), (2, step2), (3, step3)):
            for i, block in enumerate(step):
                first = at(place + (k if i % 2 else n - k)) + i // 2 * (rows // chunks)
                pieces += [(block, first)]
        late, late_at = list(step4), at(place + n // 2)
    else:
        pieces = [(lax.all_gather(w, "seq", axis=0, tiled=True), 0)]
        late, late_at = [], 0

    gate = jnp.repeat(jnp.tanh(cross_gate), HEAD_SIZE)[None, :]
    place = jnp.stack([seq, core] + [jnp.asarray(p, jnp.int32) for p in (late_at, *[p[1] for p in pieces])])
    image = [sds((2 * tile_rows, 2 * kv_cols), F32)]
    if late:
        image.append(sds((2 * tile_rows, rows), BF16))
    image = list(call(
        functools.partial(image_kernel, len(pieces), rows if late else 0),
        tuple(image),
        (place, norm, before_mine, before_other, *[p[0] for p in pieces]),
        smem=1,
        scratch=(pltpu.VMEM((width, 2 * kv_cols), BF16),),
    ))
    turn, image[0] = lax.optimization_barrier((seq.reshape(1), image[0]))
    self_out = call(
        self_kernel,
        sds(text_query_rows.shape, F32),
        (turn, text_query_rows, text, back1, back2),
        smem=1,
    )
    return call(
        cross_kernel,
        sds(text_query_rows.shape, BF16),
        (seq.reshape(1), text_query_rows, self_out, tile_span.T, gate, *image, *late),
        smem=1,
        stored=True,
        scratch=(
            pltpu.VMEM((2 * tile_rows, 2 * kv_cols), BF16),
            pltpu.VMEM(text_query_rows.shape, BF16),
            pltpu.SemaphoreType.DMA((kv_heads,)),
        ),
    )


def solution(mesh):
    placed = (
        P(("groups", "seq"), "head"),
        P(None, ("groups", "seq"), "head"),
        P(("groups", "seq")),
        P(("groups", "seq"), None),
        P(("groups", "seq"), None),
        P(None, ("groups", "seq"), "head"),
        P("head", None),
        P("seq", None, "head"),
        P("head"),
    )
    return jax.shard_map(
        per_device,
        mesh=mesh,
        in_specs=placed,
        out_specs=P(("groups", "seq"), "head"),
        check_vma=False,
    )
```
